512 devices in a mesh: tile: 128 (over y, z_hi, x), mem: 4 (over z_lo, core).
Axes of the slice: x: 4, y: 8, z: 8 (z_hi: 4, z_lo: 2; z = z_hi * 2 + z_lo), core: 2. Of those that a mesh axis runs over, the one named last changes fastest.
Arguments:
- control_ens: float32 [32, 2, 32, 16384], P('mem', None, None, 'tile'), may hold values from -1.75 to 1.75
- control_static: float32 [2, 32, 16384], P(None, None, 'tile'), may hold values from -1.75 to 1.75
- static_sigma: float32 [2, 32, 16384], P(None, None, 'tile'), may hold values from 0.5 to 2
- east_coef: float32 [2, 32, 16384], P(None, None, 'tile'), may hold values from 0.04 to 0.22
- north_coef: float32 [2, 32, 16384], P(None, None, 'tile'), may hold values from 0.04 to 0.22
- perturbations: bfloat16 [32, 4, 2, 32, 16384], P('mem', None, None, None, 'tile'), may hold values from -6 to 6
- obs_counts: int32 [4, 128, 128], P('mem', 'tile'), may hold values from 0 to 4, as said below
- obs_rows: int32 [4, 128, 128, 4], P('mem', 'tile'), may hold values from 0 to 255
- footprints: bfloat16 [4, 128, 128, 4, 128], P('mem', 'tile'), may hold values from -1.5 to 1.5
- obs_values: float32 [4, 128, 128, 4], P('mem', 'tile'), may hold values from -6 to 6
- obs_precision: float32 [4, 128, 128, 4], P('mem', 'tile'), may hold values from 0.25 to 2
Outputs:
- grad_ensemble: float32 [32, 2, 32, 16384], P('mem', None, None, 'tile')
- grad_static: float32 [2, 32, 16384], P(None, None, 'tile')
The draws below stay inside these ranges and needn't reach their ends.
Inputs may be any that keep to these rules, and one draw needn't show every extreme that they name: Slots c < obs_counts of a source and destination hold observations, the others are ignored; every source device fills all 4 slots to some destination.
All inputs are finite; a program needn't handle non-finite values.
Results may differ from the reference program's by a relative error of at most 0.0003.
Values may be sent and summed in bfloat16 or wider, within the bound.
No kernel may reach another device: no remote copies, remote signals or barrier semaphores. Data moves between devices by JAX's collectives and lax.ppermute only.
A program may use at most 64 MiB of HBM per device.

```python
import math
import jax
import jax.numpy as jnp
from jax import lax

CX = 128
CY = 32
LEVELS = 2
SLOTS = 4
SWEEPS = 2
CAP = 4
MEMBERS = 32
TILES = 128
SPLITS = 4
NX = 16384
NROWS = 256


def draw_obs_counts(key, part):
    key = jax.random.fold_in(key, 11)
    key_top, key_drop, key_full = jax.random.split(key, 3)
    ceiling = jax.random.randint(key_top, (1, 1, TILES), CAP // 2, CAP + 1)
    ceiling = jnp.broadcast_to(ceiling, (SPLITS, TILES, TILES))
    dropped = jax.random.randint(key_drop, (SPLITS, TILES, TILES), 0, ceiling // 2 + 1)
    counts_drawn = ceiling - dropped
    chosen = jax.random.randint(key_full, (SPLITS, TILES, 1), 0, TILES)
    column_index = jnp.arange(TILES, dtype=jnp.int32)[None, None, :]
    return jnp.where(column_index == chosen, CAP, counts_drawn).astype(jnp.int32)


def plant(values, rng, low, largest):
    index_at = [jax.random.randint(jax.random.fold_in(rng, axis), (), 0, length) for axis, length in enumerate(values.shape)]
    main_axis = values.shape.index(max(values.shape))
    next_to = index_at[:main_axis] + [(index_at[main_axis] + 1) % values.shape[main_axis]] + index_at[main_axis + 1:]
    return values.at[tuple(index_at)].set(low).at[tuple(next_to)].set(largest)


def level_of(rng, dims, cuts, smallest, top_value):
    gain = 1.0
    for dim, blocks in cuts:
        draws = jax.random.uniform(jax.random.fold_in(jax.random.fold_in(rng, 6), dim), (blocks,), jnp.float32, smallest / len(cuts), top_value / len(cuts))
        gain = gain * jnp.repeat(jnp.exp(draws), dims[dim] // blocks).reshape((-1,) + (1,) * (len(dims) - 1 - dim))
    return gain


def bell_draw(stream_key, extent, scale, limit, cuts=(), kind=jnp.bfloat16):
    gain = level_of(stream_key, extent, cuts, -0.22, 0.18) if cuts else 1.0
    entries = jax.random.normal(stream_key, extent, jnp.float32) * scale * gain
    return jnp.minimum(jnp.maximum(entries, -limit), limit).astype(kind)


def setup_inputs(seed: int = 0) -> dict:
    streams_of = jax.random.split(jax.random.key(seed), 12)
    control_ens = bell_draw(streams_of[0], (MEMBERS, LEVELS, CY, NX), 0.3, 1.75, ((0, 4), (3, 128)), jnp.float32)
    control_static = bell_draw(streams_of[1], (LEVELS, CY, NX), 0.3, 1.75, ((2, 128),), jnp.float32)
    static_sigma = jnp.clip(jnp.exp(math.log(2.0) - 1.3862944 * jax.random.uniform(streams_of[2], (LEVELS, CY, NX), jnp.float32) ** level_of(streams_of[2], (LEVELS, CY, NX), ((2, 128),), -0.2, 0.2)), 0.5, 2.0)
    east_coef = jnp.clip(jnp.exp(math.log(0.22) - 1.7047481 * jax.random.uniform(streams_of[3], (LEVELS, CY, NX), jnp.float32) ** level_of(streams_of[3], (LEVELS, CY, NX), ((2, 128),), -0.2, 0.2)), 0.04, 0.22)
    north_coef = jnp.clip(jnp.exp(math.log(0.22) - 1.7047481 * jax.random.uniform(streams_of[4], (LEVELS, CY, NX), jnp.float32) ** level_of(streams_of[4], (LEVELS, CY, NX), ((2, 128),), -0.2, 0.2)), 0.04, 0.22)
    perturbations = bell_draw(streams_of[5], (MEMBERS, SLOTS, LEVELS, CY, NX), 1.0, 6.0, ((0, 4), (4, 128)))
    obs_counts = draw_obs_counts(jax.random.fold_in(streams_of[11], 71), 0)
    obs_rows = plant(jax.random.randint(streams_of[7], (SPLITS, TILES, TILES, CAP), 0, NROWS), jax.random.fold_in(streams_of[7], 1), 0, NROWS - 1).astype(jnp.int32)
    footprints = bell_draw(streams_of[8], (SPLITS, TILES, TILES, CAP, CX), 0.25, 1.5, ((0, 4), (1, 128)))
    obs_values = bell_draw(streams_of[9], (SPLITS, TILES, TILES, CAP), 1.0, 6.0, ((0, 4), (1, 128)), jnp.float32)
    obs_precision = jnp.clip(jnp.exp(math.log(2.0) - 2.0794415 * jax.random.uniform(streams_of[10], (SPLITS, TILES, TILES, CAP), jnp.float32) ** level_of(streams_of[10], (SPLITS, TILES, TILES, CAP), ((0, 4), (1, 128)), -0.2, 0.2)), 0.25, 2.0)
    return dict(control_ens=control_ens, control_static=control_static, static_sigma=static_sigma, east_coef=east_coef, north_coef=north_coef, perturbations=perturbations, obs_counts=obs_counts, obs_rows=obs_rows, footprints=footprints, obs_values=obs_values, obs_precision=obs_precision)


def diffuse(grid_field, east_rate, north_rate):
    east_flux = east_rate * (jnp.roll(grid_field, -1, axis=-1) - grid_field)
    north_flux = north_rate[:, :-1, :] * (grid_field[..., 1:, :] - grid_field[..., :-1, :])
    zero_row = jnp.zeros_like(north_flux[..., :1, :])
    upper_flux = jnp.concatenate([north_flux, zero_row], axis=-2)
    lower_flux = jnp.concatenate([zero_row, north_flux], axis=-2)
    return grid_field + (east_flux - jnp.roll(east_flux, 1, axis=-1) + (upper_flux - lower_flux))

def smooth(grid_field, east_rate, north_rate):
    for sweep_index in range(SWEEPS):
        grid_field = diffuse(grid_field, east_rate, north_rate)
    return grid_field

def reference(control_ens, control_static, static_sigma, east_coef, north_coef, perturbations, obs_counts, obs_rows, footprints, obs_values, obs_precision):
    scale_ens = 1.0 / math.sqrt(MEMBERS - 1)
    stacked = jnp.concatenate([control_ens, control_static[None]], axis=0)
    smoothed = smooth(stacked, east_coef, north_coef)

    def add_member(running, inputs):
        member_pert, member_field = inputs
        return (running + member_pert.astype(jnp.float32) * member_field[None], None)
    start = jnp.zeros((SLOTS, LEVELS, CY, NX), jnp.float32)
    ens_sum, unused = lax.scan(add_member, start, (perturbations, smoothed[:-1]))
    increment = scale_ens * ens_sum + static_sigma * smoothed[-1][None]
    tables = increment.reshape(SLOTS, LEVELS, CY, TILES, CX).transpose(3, 0, 1, 2, 4).reshape(TILES, NROWS, CX)
    slot_index = jnp.arange(CAP, dtype=jnp.int32)
    live_slot = slot_index[None, None, None, :] < obs_counts[..., None]
    destination = jnp.broadcast_to(jnp.arange(TILES, dtype=jnp.int32)[None, None, :, None], obs_rows.shape)
    picked = tables[destination, obs_rows]
    weights_f = footprints.astype(jnp.float32)
    model_obs = lax.optimization_barrier(jnp.sum(weights_f * picked, axis=-1))
    residual = jnp.where(live_slot, obs_precision, 0.0) * (model_obs - obs_values)
    grad_tables = jnp.zeros((TILES, NROWS, CX), jnp.float32).at[destination, obs_rows].add(residual[..., None] * weights_f)
    gradient = grad_tables.reshape(TILES, SLOTS, LEVELS, CY, CX).transpose(1, 2, 3, 0, 4).reshape(SLOTS, LEVELS, CY, NX)

    def member_source(unused_carry, member_pert):
        return (unused_carry, scale_ens * lax.optimization_barrier(jnp.sum(member_pert.astype(jnp.float32) * gradient, axis=0)))
    unused_carry, ens_source = lax.scan(member_source, jnp.zeros((), jnp.float32), perturbations)
    static_source = static_sigma * lax.optimization_barrier(jnp.sum(gradient, axis=0))
    smoothed_back = smooth(jnp.concatenate([ens_source, static_source[None]], axis=0), east_coef, north_coef)
    return (smoothed_back[:-1] + control_ens, smoothed_back[-1] + control_static)
```

```python
import math

import jax
import jax.numpy as jnp
from jax import lax
from jax.experimental import pallas as pl
from jax.experimental.pallas import tpu as pltpu
from jax.sharding import PartitionSpec as P

SWEEPS = 2
F32 = jnp.float32
BF16 = jnp.bfloat16
VMEM = pl.BlockSpec(memory_space=pltpu.VMEM)


def call(body, out, flops, traffic, *operands):
    return pl.pallas_call(
        body,
        out_shape=out,
        in_specs=[VMEM] * len(operands),
        out_specs=jax.tree.map(lambda _: VMEM, out),
        cost_estimate=pl.CostEstimate(flops=int(flops), bytes_accessed=int(traffic), transcendentals=0),
        compiler_params=pltpu.CompilerParams(vmem_limit_bytes=32 * 1024 * 1024),
    )(*operands)


def shape(dims, kind=F32):
    return jax.ShapeDtypeStruct(dims, kind)


def shifted(x, axis, by):
    count = lax.axis_size(axis)
    return lax.ppermute(x, axis, [(i, (i + by) % count) for i in range(count)])


def everyone(copies):
    return lax.all_to_all(copies, "mem", split_axis=0, concat_axis=0, tiled=True)


def split_two(x):
    high = x.astype(BF16)
    return high, (x - high.astype(F32)).astype(BF16)


def split_three(x):
    high = x.astype(BF16)
    rest = x - high.astype(F32)
    mid = rest.astype(BF16)
    return high, mid, (rest - mid.astype(F32)).astype(BF16)


def pack_edges(fields, east_ref, west_ref):
    rows, columns = fields[0].shape
    lane = lax.broadcasted_iota(jnp.int32, (rows, columns), 1)
    east = jnp.zeros((rows, columns), F32)
    west = jnp.zeros((rows, columns), F32)
    for f, u in enumerate(fields):
        here = (lane == 2 * f) | (lane == 2 * f + 1)
        east = jnp.where(here, pltpu.roll(u, (2 * f + 2) % columns, 1), east)
        west = jnp.where(here, pltpu.roll(u, 2 * f, 1) if f else u, west)
    east_ref[...] = east
    west_ref[...] = west


def unpack_edges(from_west, from_east, f, lane):
    columns = from_west.shape[1]
    left = pltpu.roll(from_west, columns - 2 - 2 * f, 1)
    right = pltpu.roll(from_east, (columns - 2 * f) % columns, 1) if f else from_east
    return jnp.where(lane >= columns - 2, left, jnp.where(lane < 2, right, 0.0))


def diffuse(u, h, e, eh, n, nh, lane):
    rows, columns = u.shape

    def pair_roll(a, b, by, edge):
        ra, rb = pltpu.roll(a, by, 1), pltpu.roll(b, by, 1)
        at = lane == edge
        return jnp.where(at, rb, ra), jnp.where(at, ra, rb)

    ue, he = pair_roll(u, h, columns - 1, columns - 1)
    flux, flux_h = e * (ue - u), eh * (he - h)
    west, west_h = pair_roll(flux, flux_h, 1, 0)

    def vertical(a, c):
        up = c * (pltpu.roll(a, rows - 1, 0) - a)
        return up - pltpu.roll(up, 1, 0)

    return (
        u + ((flux - west) + vertical(u, n)),
        h + ((flux_h - west_h) + vertical(h, nh)),
    )


def coefficients(e_ref, n_ref, from_west, from_east, fields, lane, latitudes):
    e, n = e_ref[...], n_ref[...]
    eh = unpack_edges(from_west, from_east, fields, lane)
    nh = unpack_edges(from_west, from_east, fields + 1, lane)
    row = lax.broadcasted_iota(jnp.int32, e.shape, 0)
    last = (row & (latitudes - 1)) == latitudes - 1
    return e, eh, jnp.where(last, 0.0, n), jnp.where(last, 0.0, nh)


def edges_body(ens_ref, static_ref, e_ref, n_ref, east_ref, west_ref):
    fields = [ens_ref[m] for m in range(ens_ref.shape[0])]
    pack_edges(fields + [static_ref[...], e_ref[...], n_ref[...]], east_ref, west_ref)


def message_body(fp_ref, counts_ref, rows_ref, values_ref, precision_ref, out_ref):
    cap, dests = rows_ref.shape
    slot = lax.broadcasted_iota(jnp.int32, (cap, dests), 0)
    live = slot < counts_ref[...]
    items = [rows_ref[...].astype(F32)]
    items += [x.astype(F32) for x in split_three(values_ref[...])]
    items += [x.astype(F32) for x in split_three(jnp.where(live, precision_ref[...], 0.0))]
    items += [jnp.zeros((cap, dests), F32)]
    stacked = [x[c : c + 1] for c in range(cap) for x in items]
    stacked.append(jnp.zeros((out_ref.shape[2] - len(stacked), dests), F32))
    meta = jnp.concatenate(stacked, axis=0).T
    place = lax.broadcasted_iota(jnp.int32, out_ref.shape, 1)
    out_ref[...] = jnp.where(
        place == cap, meta[:, None, :], fp_ref[...].astype(F32)
    ).astype(BF16)


def increment_body(latitudes, scale, share, ens_ref, static_ref, sigma_ref, e_ref, n_ref, pert_ref, west_ref, east_ref, out_ref):
    members, slots = pert_ref.shape[:2]
    rows = e_ref.shape[0]
    lane = lax.broadcasted_iota(jnp.int32, e_ref.shape, 1)
    from_west, from_east = west_ref[...], east_ref[...]
    coef = coefficients(e_ref, n_ref, from_west, from_east, members + 1, lane, latitudes)

    def smooth(u, f):
        h = unpack_edges(from_west, from_east, f, lane)
        for _ in range(SWEEPS):
            u, h = diffuse(u, h, *coef, lane)
        return u

    total = [jnp.zeros(e_ref.shape, F32) for _ in range(slots)]
    for m in range(members):
        u = smooth(ens_ref[m], m)
        for t in range(slots):
            total[t] = total[t] + pert_ref[m, t].astype(F32) * u
    static = (share * sigma_ref[...]) * smooth(static_ref[...], members)
    for t in range(slots):
        part = scale * total[t] + static
        for g in range(out_ref.shape[0]):
            out_ref[g, t * rows : (t + 1) * rows, :] = part


def observe_body(cap, parts_ref, seen_ref, out_ref):
    table = parts_ref[0]
    for g in range(1, parts_ref.shape[0]):
        table = table + parts_ref[g]
    rows, columns = table.shape
    high, low = split_two(table)
    seen = seen_ref[...]
    count = seen.shape[0]
    room = seen.shape[0] // seen_ref.shape[0]
    group = 8
    eye_shape = (group * cap, columns)
    eye = (
        lax.broadcasted_iota(jnp.int32, eye_shape, 0) == lax.broadcasted_iota(jnp.int32, eye_shape, 1)
    ).astype(F32).astype(BF16)
    contract = (((1,), (1,)), ((), ()))
    got = lax.dot_general(high, seen, contract, preferred_element_type=F32)
    got = got + lax.dot_general(low, seen, contract, preferred_element_type=F32)
    meta = lax.dot_general(eye, seen, contract, preferred_element_type=F32)
    place = lax.broadcasted_iota(jnp.int32, (group, count), 1) & (group - 1)
    facts = jnp.zeros((group, count), F32)
    for c in range(cap):
        part = pltpu.roll(meta[c * group : (c + 1) * group], count - (cap - c), 1)
        facts = jnp.where(place == c, part, facts)
    row_of = jnp.where(place[:1] < cap, facts[0:1], -1.0).astype(jnp.int32)
    value = (facts[1:2] + facts[2:3]) + facts[3:4]
    precision = (facts[4:5] + facts[5:6]) + facts[6:7]
    hit = lax.broadcasted_iota(jnp.int32, (rows, count), 0) == row_of
    model = jnp.sum(jnp.where(hit, got, 0.0), axis=0, keepdims=True)
    residual = precision * (model - value)
    out = None
    for piece in split_two(residual):
        spread = jnp.where(hit, piece.astype(F32), 0.0).astype(BF16)
        term = jnp.dot(spread, seen, preferred_element_type=F32)
        out = term if out is None else out + term
    for g in range(out_ref.shape[0]):
        out_ref[g] = out


def source_body(scale, parts_ref, pert_ref, sigma_ref, out_ref, east_ref, west_ref):
    members, slots, rows = pert_ref.shape[:3]
    gradient = []
    for t in range(slots):
        span = slice(t * rows, (t + 1) * rows)
        g = parts_ref[0, span, :]
        for k in range(1, parts_ref.shape[0]):
            g = g + parts_ref[k, span, :]
        gradient.append(g)
    fields = []
    for m in range(members):
        u = pert_ref[m, 0].astype(F32) * gradient[0]
        for t in range(1, slots):
            u = u + pert_ref[m, t].astype(F32) * gradient[t]
        u = scale * u
        out_ref[m] = u
        fields.append(u)
    u = gradient[0]
    for t in range(1, slots):
        u = u + gradient[t]
    u = sigma_ref[...] * u
    out_ref[members] = u
    pack_edges(fields + [u], east_ref, west_ref)


def result_body(latitudes, source_ref, ens_ref, static_ref, e_ref, n_ref, west0_ref, east0_ref, west_ref, east_ref, ens_out, static_out):
    members = ens_ref.shape[0]
    lane = lax.broadcasted_iota(jnp.int32, e_ref.shape, 1)
    coef = coefficients(e_ref, n_ref, west0_ref[...], east0_ref[...], members + 1, lane, latitudes)
    from_west, from_east = west_ref[...], east_ref[...]
    for f in range(members + 1):
        u = source_ref[f]
        h = unpack_edges(from_west, from_east, f, lane)
        for _ in range(SWEEPS):
            u, h = diffuse(u, h, *coef, lane)
        if f < members:
            ens_out[f] = u + ens_ref[f]
        else:
            static_out[...] = u + static_ref[...]


def on_device(
    control_ens,
    control_static,
    static_sigma,
    east_coef,
    north_coef,
    perturbations,
    obs_counts,
    obs_rows,
    footprints,
    obs_values,
    obs_precision,
):
    members, levels, latitudes, columns = control_ens.shape
    slots = perturbations.shape[1]
    rows = levels * latitudes
    table_rows = slots * rows
    groups = lax.axis_size("mem")
    scale = 1.0 / math.sqrt(members * groups - 1)
    ens = control_ens.reshape(members, rows, columns)
    static = control_static.reshape(rows, columns)
    sigma = static_sigma.reshape(rows, columns)
    e = east_coef.reshape(rows, columns)
    n = north_coef.reshape(rows, columns)
    pert = perturbations.reshape(members, slots, rows, columns)
    tiles, cap = obs_rows.shape[2:]

    field = shape((rows, columns))
    to_east, to_west = call(edges_body, (field, field), 1e6, 2e6, ens, static, e, n)
    west0 = shifted(to_east, "tile", 1)
    east0 = shifted(to_west, "tile", -1)

    room = 8
    padded = jnp.pad(footprints[0, 0], ((0, 0), (0, room - cap), (0, 0)))
    message = call(
        message_body,
        shape((tiles, room, columns), BF16),
        1e6,
        1e6,
        padded,
        obs_counts[0],
        obs_rows[0, 0].T,
        obs_values[0, 0].T,
        obs_precision[0, 0].T,
    )
    seen = lax.all_to_all(message, "tile", split_axis=0, concat_axis=0, tiled=True)

    partial = call(
        lambda *refs: increment_body(latitudes, scale, 1.0 / groups, *refs),
        shape((groups, table_rows, columns)),
        1e7,
        4e6,
        ens,
        static,
        sigma,
        e,
        n,
        pert,
        west0,
        east0,
    )
    parts = everyone(partial)
    partial_grad = call(
        lambda *refs: observe_body(cap, *refs),
        shape((groups, table_rows, columns)),
        3e8,
        4e6,
        parts,
        seen.reshape(tiles * room, columns),
    )
    grad_parts = everyone(partial_grad)
    source, to_east, to_west = call(
        lambda *refs: source_body(scale, *refs),
        (shape((members + 1, rows, columns)), field, field),
        1e7,
        2e6,
        grad_parts,
        pert,
        sigma,
    )
    west1 = shifted(to_east, "tile", 1)
    east1 = shifted(to_west, "tile", -1)
    ens_out, static_out = call(
        lambda *refs: result_body(latitudes, *refs),
        (shape(ens.shape), field),
        1e7,
        2e6,
        source,
        ens,
        static,
        e,
        n,
        west0,
        east0,
        west1,
        east1,
    )
    return ens_out.reshape(control_ens.shape), static_out.reshape(control_static.shape)


def solution(mesh):
    placed = (
        P("mem", None, None, "tile"),
        P(None, None, "tile"),
        P(None, None, "tile"),
        P(None, None, "tile"),
        P(None, None, "tile"),
        P("mem", None, None, None, "tile"),
        P("mem", "tile", None),
        P("mem", "tile", None, None),
        P("mem", "tile", None, None, None),
        P("mem", "tile", None, None),
        P("mem", "tile", None, None),
    )
    return jax.shard_map(
        on_device,
        mesh=mesh,
        in_specs=placed,
        out_specs=(P("mem", None, None, "tile"), P(None, None, "tile")),
        check_vma=False,
    )
```

```python
import math

import jax
import jax.numpy as jnp
from jax import lax
from jax.experimental import pallas as pl
from jax.experimental.pallas import tpu as pltpu
from jax.sharding import PartitionSpec as P

SWEEPS = 2
F32 = jnp.float32
BF16 = jnp.bfloat16
VMEM = pl.BlockSpec(memory_space=pltpu.VMEM)


def call(body, out, flops, traffic, *operands):
    return pl.pallas_call(
        body,
        out_shape=out,
        in_specs=[VMEM] * len(operands),
        out_specs=jax.tree.map(lambda _: VMEM, out),
        cost_estimate=pl.CostEstimate(flops=int(flops), bytes_accessed=int(traffic), transcendentals=0),
        compiler_params=pltpu.CompilerParams(vmem_limit_bytes=32 * 1024 * 1024),
    )(*operands)


def shape(dims, kind=F32):
    return jax.ShapeDtypeStruct(dims, kind)


def shifted(x, axis, by):
    count = lax.axis_size(axis)
    return lax.ppermute(x, axis, [(i, (i + by) % count) for i in range(count)])


def split_two(x):
    high = x.astype(BF16)
    return high, (x - high.astype(F32)).astype(BF16)


def split_three(x):
    high = x.astype(BF16)
    rest = x - high.astype(F32)
    mid = rest.astype(BF16)
    return high, mid, (rest - mid.astype(F32)).astype(BF16)


def pack_edges(fields, east_ref, west_ref):
    rows, columns = fields[0].shape
    lane = lax.broadcasted_iota(jnp.int32, (rows, columns), 1)
    east = jnp.zeros((rows, columns), F32)
    west = jnp.zeros((rows, columns), F32)
    for f, u in enumerate(fields):
        here = (lane == 2 * f) | (lane == 2 * f + 1)
        east = jnp.where(here, pltpu.roll(u, (2 * f + 2) % columns, 1), east)
        west = jnp.where(here, pltpu.roll(u, 2 * f, 1) if f else u, west)
    east_ref[...] = east
    west_ref[...] = west


def unpack_edges(from_west, from_east, f, lane):
    columns = from_west.shape[1]
    left = pltpu.roll(from_west, columns - 2 - 2 * f, 1)
    right = pltpu.roll(from_east, (columns - 2 * f) % columns, 1) if f else from_east
    return jnp.where(lane >= columns - 2, left, jnp.where(lane < 2, right, 0.0))


def diffuse(u, h, e, eh, n, nh, lane):
    rows, columns = u.shape

    def pair_roll(a, b, by, edge):
        ra, rb = pltpu.roll(a, by, 1), pltpu.roll(b, by, 1)
        at = lane == edge
        return jnp.where(at, rb, ra), jnp.where(at, ra, rb)

    ue, he = pair_roll(u, h, columns - 1, columns - 1)
    flux, flux_h = e * (ue - u), eh * (he - h)
    west, west_h = pair_roll(flux, flux_h, 1, 0)

    def vertical(a, c):
        up = c * (pltpu.roll(a, rows - 1, 0) - a)
        return up - pltpu.roll(up, 1, 0)

    return (
        u + ((flux - west) + vertical(u, n)),
        h + ((flux_h - west_h) + vertical(h, nh)),
    )


def coefficients(e_ref, n_ref, from_west, from_east, fields, lane, latitudes):
    e, n = e_ref[...], n_ref[...]
    eh = unpack_edges(from_west, from_east, fields, lane)
    nh = unpack_edges(from_west, from_east, fields + 1, lane)
    row = lax.broadcasted_iota(jnp.int32, e.shape, 0)
    last = (row & (latitudes - 1)) == latitudes - 1
    return e, eh, jnp.where(last, 0.0, n), jnp.where(last, 0.0, nh)


def edges_body(ens_ref, static_ref, e_ref, n_ref, east_ref, west_ref):
    fields = [ens_ref[m] for m in range(ens_ref.shape[0])]
    pack_edges(fields + [static_ref[...], e_ref[...], n_ref[...]], east_ref, west_ref)


def message_body(fp_ref, counts_ref, rows_ref, values_ref, precision_ref, out_ref):
    cap, dests = rows_ref.shape
    slot = lax.broadcasted_iota(jnp.int32, (cap, dests), 0)
    live = slot < counts_ref[...]
    items = [rows_ref[...].astype(F32)]
    items += [x.astype(F32) for x in split_three(values_ref[...])]
    items += [x.astype(F32) for x in split_three(jnp.where(live, precision_ref[...], 0.0))]
    items += [jnp.zeros((cap, dests), F32)]
    stacked = [x[c : c + 1] for c in range(cap) for x in items]
    stacked.append(jnp.zeros((out_ref.shape[2] - len(stacked), dests), F32))
    meta = jnp.concatenate(stacked, axis=0).T
    place = lax.broadcasted_iota(jnp.int32, out_ref.shape, 1)
    out_ref[...] = jnp.where(
        place == cap, meta[:, None, :], fp_ref[...].astype(F32)
    ).astype(BF16)


def increment_body(latitudes, scale, share, ens_ref, static_ref, sigma_ref, e_ref, n_ref, pert_ref, west_ref, east_ref, out_ref):
    members, slots = pert_ref.shape[:2]
    rows = e_ref.shape[0]
    lane = lax.broadcasted_iota(jnp.int32, e_ref.shape, 1)
    from_west, from_east = west_ref[...], east_ref[...]
    coef = coefficients(e_ref, n_ref, from_west, from_east, members + 1, lane, latitudes)

    def smooth(u, f):
        h = unpack_edges(from_west, from_east, f, lane)
        for _ in range(SWEEPS):
            u, h = diffuse(u, h, *coef, lane)
        return u

    total = [jnp.zeros(e_ref.shape, F32) for _ in range(slots)]
    for m in range(members):
        u = smooth(ens_ref[m], m)
        for t in range(slots):
            total[t] = total[t] + pert_ref[m, t].astype(F32) * u
    static = (share * sigma_ref[...]) * smooth(static_ref[...], members)
    for t in range(slots):
        part = scale * total[t] + static
        out_ref[t * rows : (t + 1) * rows, :] = part


def observe_body(cap, parts_ref, seen_ref, out_ref):
    table = parts_ref[0]
    for g in range(1, parts_ref.shape[0]):
        table = table + parts_ref[g]
    rows, columns = table.shape
    high, low = split_two(table)
    seen = seen_ref[...]
    count = seen.shape[0]
    room = seen.shape[0] // seen_ref.shape[0]
    group = 8
    eye_shape = (group * cap, columns)
    eye = (
        lax.broadcasted_iota(jnp.int32, eye_shape, 0) == lax.broadcasted_iota(jnp.int32, eye_shape, 1)
    ).astype(F32).astype(BF16)
    contract = (((1,), (1,)), ((), ()))
    got = lax.dot_general(high, seen, contract, preferred_element_type=F32)
    got = got + lax.dot_general(low, seen, contract, preferred_element_type=F32)
    meta = lax.dot_general(eye, seen, contract, preferred_element_type=F32)
    place = lax.broadcasted_iota(jnp.int32, (group, count), 1) & (group - 1)
    facts = jnp.zeros((group, count), F32)
    for c in range(cap):
        part = pltpu.roll(meta[c * group : (c + 1) * group], count - (cap - c), 1)
        facts = jnp.where(place == c, part, facts)
    row_of = jnp.where(place[:1] < cap, facts[0:1], -1.0).astype(jnp.int32)
    value = (facts[1:2] + facts[2:3]) + facts[3:4]
    precision = (facts[4:5] + facts[5:6]) + facts[6:7]
    hit = lax.broadcasted_iota(jnp.int32, (rows, count), 0) == row_of
    model = jnp.sum(jnp.where(hit, got, 0.0), axis=0, keepdims=True)
    residual = precision * (model - value)
    out = None
    for piece in split_two(residual):
        spread = jnp.where(hit, piece.astype(F32), 0.0).astype(BF16)
        term = jnp.dot(spread, seen, preferred_element_type=F32)
        out = term if out is None else out + term
    out_ref[...] = out


def source_body(scale, parts_ref, pert_ref, sigma_ref, out_ref, east_ref, west_ref):
    members, slots, rows = pert_ref.shape[:3]
    gradient = []
    for t in range(slots):
        span = slice(t * rows, (t + 1) * rows)
        g = parts_ref[0, span, :]
        for k in range(1, parts_ref.shape[0]):
            g = g + parts_ref[k, span, :]
        gradient.append(g)
    fields = []
    for m in range(members):
        u = pert_ref[m, 0].astype(F32) * gradient[0]
        for t in range(1, slots):
            u = u + pert_ref[m, t].astype(F32) * gradient[t]
        u = scale * u
        out_ref[m] = u
        fields.append(u)
    u = gradient[0]
    for t in range(1, slots):
        u = u + gradient[t]
    u = sigma_ref[...] * u
    out_ref[members] = u
    pack_edges(fields + [u], east_ref, west_ref)


def result_body(latitudes, source_ref, ens_ref, static_ref, e_ref, n_ref, west0_ref, east0_ref, west_ref, east_ref, ens_out, static_out):
    members = ens_ref.shape[0]
    lane = lax.broadcasted_iota(jnp.int32, e_ref.shape, 1)
    coef = coefficients(e_ref, n_ref, west0_ref[...], east0_ref[...], members + 1, lane, latitudes)
    from_west, from_east = west_ref[...], east_ref[...]
    for f in range(members + 1):
        u = source_ref[f]
        h = unpack_edges(from_west, from_east, f, lane)
        for _ in range(SWEEPS):
            u, h = diffuse(u, h, *coef, lane)
        if f < members:
            ens_out[f] = u + ens_ref[f]
        else:
            static_out[...] = u + static_ref[...]


def on_device(
    control_ens,
    control_static,
    static_sigma,
    east_coef,
    north_coef,
    perturbations,
    obs_counts,
    obs_rows,
    footprints,
    obs_values,
    obs_precision,
):
    members, levels, latitudes, columns = control_ens.shape
    slots = perturbations.shape[1]
    rows = levels * latitudes
    table_rows = slots * rows
    groups = lax.axis_size("mem")
    scale = 1.0 / math.sqrt(members * groups - 1)
    ens = control_ens.reshape(members, rows, columns)
    static = control_static.reshape(rows, columns)
    sigma = static_sigma.reshape(rows, columns)
    e = east_coef.reshape(rows, columns)
    n = north_coef.reshape(rows, columns)
    pert = perturbations.reshape(members, slots, rows, columns)
    tiles, cap = obs_rows.shape[2:]

    field = shape((rows, columns))
    to_east, to_west = call(edges_body, (field, field), 1e6, 2e6, ens, static, e, n)
    west0 = shifted(to_east, "tile", 1)
    east0 = shifted(to_west, "tile", -1)

    room = 8
    padded = jnp.pad(footprints[0, 0], ((0, 0), (0, room - cap), (0, 0)))
    message = call(
        message_body,
        shape((tiles, room, columns), BF16),
        1e6,
        1e6,
        padded,
        obs_counts[0],
        obs_rows[0, 0].T,
        obs_values[0, 0].T,
        obs_precision[0, 0].T,
    )
    seen = lax.all_to_all(message, "tile", split_axis=0, concat_axis=0, tiled=True)

    partial = call(
        lambda *refs: increment_body(latitudes, scale, 1.0 / groups, *refs),
        shape((table_rows, columns)),
        1e7,
        4e6,
        ens,
        static,
        sigma,
        e,
        n,
        pert,
        west0,
        east0,
    )
    parts = lax.all_gather(partial, "mem")
    partial_grad = call(
        lambda *refs: observe_body(cap, *refs),
        shape((table_rows, columns)),
        3e8,
        4e6,
        parts,
        seen.reshape(tiles * room, columns),
    )
    grad_parts = lax.all_gather(partial_grad, "mem")
    source, to_east, to_west = call(
        lambda *refs: source_body(scale, *refs),
        (shape((members + 1, rows, columns)), field, field),
        1e7,
        2e6,
        grad_parts,
        pert,
        sigma,
    )
    west1 = shifted(to_east, "tile", 1)
    east1 = shifted(to_west, "tile", -1)
    ens_out, static_out = call(
        lambda *refs: result_body(latitudes, *refs),
        (shape(ens.shape), field),
        1e7,
        2e6,
        source,
        ens,
        static,
        e,
        n,
        west0,
        east0,
        west1,
        east1,
    )
    return ens_out.reshape(control_ens.shape), static_out.reshape(control_static.shape)


def solution(mesh):
    placed = (
        P("mem", None, None, "tile"),
        P(None, None, "tile"),
        P(None, None, "tile"),
        P(None, None, "tile"),
        P(None, None, "tile"),
        P("mem", None, None, None, "tile"),
        P("mem", "tile", None),
        P("mem", "tile", None, None),
        P("mem", "tile", None, None, None),
        P("mem", "tile", None, None),
        P("mem", "tile", None, None),
    )
    return jax.shard_map(
        on_device,
        mesh=mesh,
        in_specs=placed,
        out_specs=(P("mem", None, None, "tile"), P(None, None, "tile")),
        check_vma=False,
    )
```

```python
import math

import jax
import jax.numpy as jnp
from jax import lax
from jax.experimental import pallas as pl
from jax.experimental.pallas import tpu as pltpu
from jax.sharding import PartitionSpec as P

SWEEPS = 2
F32 = jnp.float32
BF16 = jnp.bfloat16
BESIDE = 1e9
RUN = 4
VMEM = pl.BlockSpec(memory_space=pltpu.VMEM)
BLOCKS = pl.BlockSpec()


def call(body, out, flops, traffic, *operands, spec=VMEM, limit=32):
    return pl.pallas_call(
        body,
        out_shape=out,
        in_specs=[spec] * len(operands),
        out_specs=jax.tree.map(lambda _: VMEM, out),
        cost_estimate=pl.CostEstimate(flops=int(flops), bytes_accessed=int(traffic), transcendentals=0),
        compiler_params=pltpu.CompilerParams(vmem_limit_bytes=limit * 1024 * 1024),
    )(*operands)


def shape(dims, kind=F32):
    return jax.ShapeDtypeStruct(dims, kind)


def from_neighbours(x, axis):
    count = lax.axis_size(axis)
    swaps = []
    for start in (1, 0):
        pairs = [(i % count, (i + 1) % count) for i in range(start, count + start, 2)]
        swaps.append(lax.ppermute(x, axis, pairs + [(j, i) for i, j in pairs]))
    odd = lax.axis_index(axis) % 2 == 1
    return jnp.where(odd, swaps[1], swaps[0]), jnp.where(odd, swaps[0], swaps[1])


def spread(x, axis):
    count = lax.axis_size(axis)
    inner, outer = x.shape[:2]
    runs = [[o * inner + i for i in range(inner)] for o in range(outer)]
    across = [[o * inner + i for o in range(outer)] for i in range(inner)]
    x = lax.all_to_all(x, axis, 0, 0, axis_index_groups=runs, tiled=True)
    x = jnp.swapaxes(x, 0, 1)
    x = lax.all_to_all(x, axis, 0, 0, axis_index_groups=across, tiled=True)
    return x.reshape(count, *x.shape[2:])


def split_two(x):
    high = x.astype(BF16)
    return high, (x - high.astype(F32)).astype(BF16)


def split_three(x):
    high = x.astype(BF16)
    rest = x - high.astype(F32)
    mid = rest.astype(BF16)
    return high, mid, (rest - mid.astype(F32)).astype(BF16)


WIDE = 12
EDGE = 2


def lanes_of(dims):
    return lax.broadcasted_iota(jnp.int32, dims, 1)


def turn(x, by):
    by = by % x.shape[1]
    return pltpu.roll(x, by, 1) if by else x


def between(lane, low, high):
    return (lane >= low) & (lane < high)


def own_edges(x, start, keep, lane, packed):
    columns = x.shape[1]
    packed = jnp.where(between(lane, start, start + keep), turn(x, start), packed)
    end = start + 2 * keep
    return jnp.where(between(lane, start + keep, end), turn(x, end - columns), packed)


def pack_fields(fields):
    packed = jnp.zeros(fields[0].shape, F32)
    lane = lanes_of(packed.shape)
    for f, u in enumerate(fields):
        packed = own_edges(u, WIDE * f + EDGE, WIDE // 2 - EDGE, lane, packed)
    return packed


def place_edges(packed, f, lane):
    columns = packed.shape[1]
    start = WIDE * f + EDGE
    left = turn(packed, -start)
    right = turn(packed, columns - (WIDE * (f + 1) - EDGE))
    return jnp.where(lane < EDGE, left, right)


def at_edge(lane, columns):
    return (lane < EDGE) | (lane >= columns - EDGE)


def diffuse(u, e, n):
    rows = u.shape[0]
    flux = e * (turn(u, -1) - u)
    up = n * (pltpu.roll(u, rows - 1, 0) - u)
    return u + ((flux - turn(flux, 1)) + (up - pltpu.roll(up, 1, 0)))


def smooth(u, e, n):
    for _ in range(SWEEPS):
        u = diffuse(u, e, n)
    return u


def closed(n, latitudes):
    row = lax.broadcasted_iota(jnp.int32, n.shape, 0)
    return jnp.where((row & (latitudes - 1)) == latitudes - 1, 0.0, n)


def with_neighbours(own, from_west, from_east, fields, lane):
    at = lane % WIDE
    west = (at < EDGE) & (lane < WIDE * fields)
    east = (at >= WIDE - EDGE) & (lane < WIDE * fields)
    out = jnp.where(west, turn(from_west, 2 * EDGE - WIDE), own)
    return jnp.where(east, turn(from_east, WIDE - 2 * EDGE), out)


def repeated(first, count, lane):
    out, have = first, 1
    while have < count:
        out = jnp.where(lane < WIDE * have, out, turn(out, WIDE * have))
        have *= 2
    return out


def edges_body(ens_ref, static_ref, e_ref, n_ref, out_ref):
    members = ens_ref.shape[0]
    packed = pack_fields([ens_ref[m] for m in range(members)] + [static_ref[...], e_ref[...]])
    start = WIDE * (members + 2)
    out_ref[...] = own_edges(n_ref[...], start, EDGE, lanes_of(packed.shape), packed)


def message_body(fp_ref, counts_ref, rows_ref, values_ref, precision_ref, out_ref):
    cap, dests = rows_ref.shape
    slot = lax.broadcasted_iota(jnp.int32, (cap, dests), 0)
    live = slot < counts_ref[...]
    items = [rows_ref[...].astype(F32)]
    items += [x.astype(F32) for x in split_three(values_ref[...])]
    items += [x.astype(F32) for x in split_three(jnp.where(live, precision_ref[...], 0.0))]
    items += [jnp.zeros((cap, dests), F32)]
    stacked = [x[c : c + 1] for c in range(cap) for x in items]
    stacked.append(jnp.zeros((out_ref.shape[3] - len(stacked), dests), F32))
    meta = jnp.concatenate(stacked, axis=0).T
    place = lax.broadcasted_iota(jnp.int32, (dests, *out_ref.shape[2:]), 1)
    fp = fp_ref[...].astype(F32)
    fp = jnp.concatenate([fp, jnp.zeros_like(fp)], axis=1)
    full = jnp.where(place == cap, meta[:, None, :], fp).astype(BF16)
    inner, outer = out_ref.shape[:2]
    full = full.reshape(outer, inner, *full.shape[1:])
    for i in range(inner):
        out_ref[i] = full[:, i]


def first_body(fp_ref, counts_ref, rows_ref, values_ref, precision_ref, ens_ref, static_ref, e_ref, n_ref, out_ref, own_ref):
    edges_body(ens_ref, static_ref, e_ref, n_ref, own_ref)
    message_body(fp_ref, counts_ref, rows_ref, values_ref, precision_ref, out_ref)


def inner_increment_body(latitudes, scale, share, ens_ref, static_ref, sigma_ref, e_ref, n_ref, pert_ref, out_ref):
    members, slots = pert_ref.shape[:2]
    rows, columns = e_ref.shape
    edge = at_edge(lanes_of(e_ref.shape), columns)
    e, n = e_ref[...], closed(n_ref[...], latitudes)
    total = [jnp.zeros(e_ref.shape, F32) for _ in range(slots)]
    for m in range(members):
        u = smooth(ens_ref[m], e, n)
        for t in range(slots):
            total[t] = total[t] + pert_ref[m, t].astype(F32) * u
    static = (share * sigma_ref[...]) * smooth(static_ref[...], e, n)
    for t in range(slots):
        out_ref[t * rows : (t + 1) * rows, :] = jnp.where(edge, 0.0, scale * total[t] + static)


def outer_increment_body(
    latitudes, scale, share, inner_ref, own_ref, west_ref, east_ref, sigma_ref, e_ref, n_ref, pert_ref, out_ref, e_out, n_out
):
    members, slots = pert_ref.shape[:2]
    rows, columns = e_ref.shape
    fields = members + 1
    lane = lanes_of(e_ref.shape)
    own, from_west, from_east = own_ref[...], west_ref[...], east_ref[...]

    def coefficient(x, west, west_at, east, east_at):
        first = own_edges(x, EDGE, WIDE // 2 - EDGE, lane, jnp.zeros(x.shape, F32))
        first = jnp.where(lane < EDGE, turn(west, -west_at), first)
        ends = WIDE - EDGE
        first = jnp.where(between(lane, ends, WIDE), turn(east, ends - east_at), first)
        return repeated(first, fields, lane)

    e_at, n_at = WIDE * fields, WIDE * (fields + 1)
    e = coefficient(e_ref[...], from_west, e_at + WIDE - 2 * EDGE, from_east, e_at + EDGE)
    n = coefficient(n_ref[...], from_west, n_at + EDGE, from_east, n_at)
    n = closed(n, latitudes)
    e_out[...] = e
    n_out[...] = n
    packed = smooth(with_neighbours(own, from_west, from_east, fields, lane), e, n)
    total = [jnp.zeros(e_ref.shape, F32) for _ in range(slots)]
    for m in range(members):
        u = place_edges(packed, m, lane)
        for t in range(slots):
            total[t] = total[t] + pert_ref[m, t].astype(F32) * u
    static = (share * sigma_ref[...]) * place_edges(packed, members, lane)
    edge = at_edge(lane, columns)
    for t in range(slots):
        span = slice(t * rows, (t + 1) * rows)
        out_ref[span, :] = jnp.where(edge, scale * total[t] + static, inner_ref[span, :])


def observe_body(cap, parts_ref, seen_ref, out_ref):
    table = parts_ref[0]
    for g in range(1, parts_ref.shape[0]):
        table = table + parts_ref[g]
    rows, columns = table.shape
    high, low = split_two(table)
    seen = seen_ref[...]
    count = seen.shape[0]
    room = seen.shape[0] // seen_ref.shape[0]
    group = 8
    eye_shape = (group * cap, columns)
    eye = (
        lax.broadcasted_iota(jnp.int32, eye_shape, 0) == lax.broadcasted_iota(jnp.int32, eye_shape, 1)
    ).astype(F32).astype(BF16)
    contract = (((1,), (1,)), ((), ()))
    got = lax.dot_general(high, seen, contract, preferred_element_type=F32)
    got = got + lax.dot_general(low, seen, contract, preferred_element_type=F32)
    meta = lax.dot_general(eye, seen, contract, preferred_element_type=F32)
    place = lax.broadcasted_iota(jnp.int32, (group, count), 1) & (group - 1)
    facts = jnp.zeros((group, count), F32)
    for c in range(cap):
        part = pltpu.roll(meta[c * group : (c + 1) * group], count - (cap - c), 1)
        facts = jnp.where(place == c, part, facts)
    row_of = jnp.where(place[:1] < cap, facts[0:1], -1.0).astype(jnp.int32)
    value = (facts[1:2] + facts[2:3]) + facts[3:4]
    precision = (facts[4:5] + facts[5:6]) + facts[6:7]
    hit = lax.broadcasted_iota(jnp.int32, (rows, count), 0) == row_of
    model = jnp.sum(jnp.where(hit, got, 0.0), axis=0, keepdims=True)
    residual = precision * (model - value)
    out = None
    for piece in split_two(residual):
        spread = jnp.where(hit, piece.astype(F32), 0.0).astype(BF16)
        term = jnp.dot(spread, seen, preferred_element_type=F32)
        out = term if out is None else out + term
    out_ref[...] = out


def source_body(scale, parts_ref, pert_ref, sigma_ref, out_ref, packed_ref):
    members, slots, rows = pert_ref.shape[:3]
    gradient = []
    for t in range(slots):
        span = slice(t * rows, (t + 1) * rows)
        g = parts_ref[0, span, :]
        for k in range(1, parts_ref.shape[0]):
            g = g + parts_ref[k, span, :]
        gradient.append(g)
    fields = []
    for m in range(members):
        u = pert_ref[m, 0].astype(F32) * gradient[0]
        for t in range(1, slots):
            u = u + pert_ref[m, t].astype(F32) * gradient[t]
        u = scale * u
        out_ref[m] = u
        fields.append(u)
    u = gradient[0]
    for t in range(1, slots):
        u = u + gradient[t]
    u = sigma_ref[...] * u
    out_ref[members] = u
    packed_ref[...] = pack_fields(fields + [u])


def inner_result_body(latitudes, source_ref, ens_ref, static_ref, e_ref, n_ref, out_ref):
    members = ens_ref.shape[0]
    e, n = e_ref[...], closed(n_ref[...], latitudes)
    for f in range(members + 1):
        out_ref[f] = smooth(source_ref[f], e, n) + (ens_ref[f] if f < members else static_ref[...])


def outer_result_body(inner_ref, own_ref, west_ref, east_ref, controls_ref, e_ref, n_ref, ens_out, static_out):
    members, _, columns = ens_out.shape
    lane = lanes_of(own_ref.shape)
    edge = at_edge(lane, columns)
    packed = with_neighbours(own_ref[...], west_ref[...], east_ref[...], members + 1, lane)
    packed = smooth(packed, e_ref[...], n_ref[...]) + controls_ref[...]
    for f in range(members + 1):
        u = jnp.where(edge, place_edges(packed, f, lane), inner_ref[f])
        if f < members:
            ens_out[f] = u
        else:
            static_out[...] = u


def on_device(
    control_ens,
    control_static,
    static_sigma,
    east_coef,
    north_coef,
    perturbations,
    obs_counts,
    obs_rows,
    footprints,
    obs_values,
    obs_precision,
):
    members, levels, latitudes, columns = control_ens.shape
    slots = perturbations.shape[1]
    rows = levels * latitudes
    table_rows = slots * rows
    groups = lax.axis_size("mem")
    scale = 1.0 / math.sqrt(members * groups - 1)
    ens = control_ens.reshape(members, rows, columns)
    static = control_static.reshape(rows, columns)
    sigma = static_sigma.reshape(rows, columns)
    e = east_coef.reshape(rows, columns)
    n = north_coef.reshape(rows, columns)
    pert = perturbations.reshape(members, slots, rows, columns)
    tiles, cap = obs_rows.shape[2:]

    field = shape((rows, columns))

    room = 8
    message, own = call(
        first_body,
        (shape((RUN, tiles // RUN, room, columns), BF16), field),
        1e6,
        1e6,
        footprints[0, 0],
        obs_counts[0],
        obs_rows[0, 0].T,
        obs_values[0, 0].T,
        obs_precision[0, 0].T,
        ens,
        static,
        e,
        n,
        spec=BLOCKS,
        limit=60,
    )
    west, east = from_neighbours(own, "tile")
    seen = spread(message, "tile")

    share = 1.0 / groups
    inner = call(
        lambda *refs: inner_increment_body(latitudes, scale, share, *refs),
        shape((table_rows, columns)),
        BESIDE,
        4e6,
        ens,
        static,
        sigma,
        e,
        n,
        pert,
    )
    partial, e_packed, n_packed = call(
        lambda *refs: outer_increment_body(latitudes, scale, share, *refs),
        (shape((table_rows, columns)), field, field),
        1e7,
        4e6,
        inner,
        own,
        west,
        east,
        sigma,
        e,
        n,
        pert,
    )
    parts = lax.all_gather(partial, "mem")
    partial_grad = call(
        lambda *refs: observe_body(cap, *refs),
        shape((table_rows, columns)),
        3e8,
        4e6,
        parts,
        seen.reshape(tiles * room, columns),
    )
    grad_parts = lax.all_gather(partial_grad, "mem")
    source, own_source = call(
        lambda *refs: source_body(scale, *refs),
        (shape((members + 1, rows, columns)), field),
        1e7,
        2e6,
        grad_parts,
        pert,
        sigma,
    )
    west, east = from_neighbours(own_source, "tile")
    inner = call(
        lambda *refs: inner_result_body(latitudes, *refs),
        shape(source.shape),
        BESIDE,
        4e6,
        source,
        ens,
        static,
        e,
        n,
    )
    ens_out, static_out = call(
        outer_result_body,
        (shape(ens.shape), field),
        1e7,
        2e6,
        inner,
        own_source,
        west,
        east,
        own,
        e_packed,
        n_packed,
    )
    return ens_out.reshape(control_ens.shape), static_out.reshape(control_static.shape)


def solution(mesh):
    placed = (
        P("mem", None, None, "tile"),
        P(None, None, "tile"),
        P(None, None, "tile"),
        P(None, None, "tile"),
        P(None, None, "tile"),
        P("mem", None, None, None, "tile"),
        P("mem", "tile", None),
        P("mem", "tile", None, None),
        P("mem", "tile", None, None, None),
        P("mem", "tile", None, None),
        P("mem", "tile", None, None),
    )
    return jax.shard_map(
        on_device,
        mesh=mesh,
        in_specs=placed,
        out_specs=(P("mem", None, None, "tile"), P(None, None, "tile")),
        check_vma=False,
    )
```

```python
import math

import jax
import jax.numpy as jnp
from jax import lax
from jax.experimental import pallas as pl
from jax.experimental.pallas import tpu as pltpu
from jax.sharding import PartitionSpec as P

SWEEPS = 2
F32 = jnp.float32
BF16 = jnp.bfloat16
BESIDE = 1e9
RUN = 4
TURN = 2e10
VMEM = pl.BlockSpec(memory_space=pltpu.VMEM)
BLOCKS = pl.BlockSpec()


def call(body, out, flops, traffic, *operands, spec=VMEM, limit=32, scratch=()):
    return pl.pallas_call(
        body,
        out_shape=out,
        in_specs=[spec] * len(operands),
        out_specs=jax.tree.map(lambda _: VMEM, out),
        scratch_shapes=scratch,
        cost_estimate=pl.CostEstimate(flops=int(flops), bytes_accessed=int(traffic), transcendentals=0),
        compiler_params=pltpu.CompilerParams(vmem_limit_bytes=limit * 1024 * 1024),
    )(*operands)


def shape(dims, kind=F32):
    return jax.ShapeDtypeStruct(dims, kind)


def from_neighbours(x, axis):
    count = lax.axis_size(axis)
    swaps = []
    for start in (1, 0):
        pairs = [(i % count, (i + 1) % count) for i in range(start, count + start, 2)]
        swaps.append(lax.ppermute(x, axis, pairs + [(j, i) for i, j in pairs]))
    odd = lax.axis_index(axis) % 2 == 1
    return jnp.where(odd, swaps[1], swaps[0]), jnp.where(odd, swaps[0], swaps[1])


def spread(x, axis, wide):
    inner, room, outer, columns = x.shape
    runs = [[o * inner + i for i in range(inner)] for o in range(outer)]
    across = [[o * inner + i for o in range(outer)] for i in range(inner)]
    x = lax.all_to_all(x, axis, 0, 0, axis_index_groups=runs, tiled=True)
    x = call(
        turn_body,
        shape((outer, wide, columns), BF16),
        TURN,
        1e6,
        x,
        scratch=[pltpu.VMEM((outer * wide, columns), F32)],
    )
    return x, lax.all_to_all(x, axis, 0, 0, axis_index_groups=across, tiled=True)


def split_two(x):
    high = x.astype(BF16)
    return high, (x - high.astype(F32)).astype(BF16)


def split_three(x):
    high = x.astype(BF16)
    rest = x - high.astype(F32)
    mid = rest.astype(BF16)
    return high, mid, (rest - mid.astype(F32)).astype(BF16)


STEPS = 256
LARGEST = 32600.0
TAIL = 16


def scale_of(steps):
    return jnp.exp2(steps * (1.0 / STEPS))


def encode(table, out_ref):
    rows, columns = table.shape
    most = jnp.max(jnp.abs(table), axis=0, keepdims=True)
    steps = jnp.ceil(jnp.log2(jnp.maximum(most, 1e-30)) * STEPS)
    coded = jnp.round(table * (LARGEST / scale_of(steps)))
    out_ref[0:rows, :] = coded.astype(jnp.int32).astype(jnp.int16)
    tail = jnp.broadcast_to(steps, (TAIL, columns))
    out_ref[rows : rows + TAIL, :] = tail.astype(jnp.int32).astype(jnp.int16)


def decode(parts_ref, low, high):
    rows = parts_ref.shape[1] - TAIL
    total = None
    for k in range(parts_ref.shape[0]):
        steps = parts_ref[k, rows : rows + TAIL, :].astype(jnp.int32).astype(F32)[0:1]
        unit = scale_of(steps) * (1.0 / LARGEST)
        part = parts_ref[k, low:high, :].astype(jnp.int32).astype(F32) * unit
        total = part if total is None else total + part
    return total


WIDE = 12
EDGE = 2


def lanes_of(dims):
    return lax.broadcasted_iota(jnp.int32, dims, 1)


def turn(x, by):
    by = by % x.shape[1]
    return pltpu.roll(x, by, 1) if by else x


def between(lane, low, high):
    return (lane >= low) & (lane < high)


def own_edges(x, start, keep, lane, packed):
    columns = x.shape[1]
    packed = jnp.where(between(lane, start, start + keep), turn(x, start), packed)
    end = start + 2 * keep
    return jnp.where(between(lane, start + keep, end), turn(x, end - columns), packed)


def pack_fields(fields):
    packed = jnp.zeros(fields[0].shape, F32)
    lane = lanes_of(packed.shape)
    for f, u in enumerate(fields):
        packed = own_edges(u, WIDE * f + EDGE, WIDE // 2 - EDGE, lane, packed)
    return packed


def place_edges(packed, f, lane):
    columns = packed.shape[1]
    start = WIDE * f + EDGE
    left = turn(packed, -start)
    right = turn(packed, columns - (WIDE * (f + 1) - EDGE))
    return jnp.where(lane < EDGE, left, right)


def at_edge(lane, columns):
    return (lane < EDGE) | (lane >= columns - EDGE)


def diffuse(u, e, n):
    rows = u.shape[0]
    flux = e * (turn(u, -1) - u)
    up = n * (pltpu.roll(u, rows - 1, 0) - u)
    return u + ((flux - turn(flux, 1)) + (up - pltpu.roll(up, 1, 0)))


def smooth(u, e, n):
    for _ in range(SWEEPS):
        u = diffuse(u, e, n)
    return u


def closed(n, latitudes):
    row = lax.broadcasted_iota(jnp.int32, n.shape, 0)
    return jnp.where((row & (latitudes - 1)) == latitudes - 1, 0.0, n)


def with_neighbours(own, from_west, from_east, fields, lane):
    at = lane % WIDE
    west = (at < EDGE) & (lane < WIDE * fields)
    east = (at >= WIDE - EDGE) & (lane < WIDE * fields)
    out = jnp.where(west, turn(from_west, 2 * EDGE - WIDE), own)
    return jnp.where(east, turn(from_east, WIDE - 2 * EDGE), out)


def repeated(first, count, lane):
    out, have = first, 1
    while have < count:
        out = jnp.where(lane < WIDE * have, out, turn(out, WIDE * have))
        have *= 2
    return out


def edges_body(ens_ref, static_ref, e_ref, n_ref, out_ref):
    members = ens_ref.shape[0]
    packed = pack_fields([ens_ref[m] for m in range(members)] + [static_ref[...], e_ref[...]])
    start = WIDE * (members + 2)
    out_ref[...] = own_edges(n_ref[...], start, EDGE, lanes_of(packed.shape), packed)


def message_body(fp_ref, counts_ref, rows_ref, values_ref, precision_ref, out_ref, full_ref):
    cap, dests = rows_ref.shape
    slot = lax.broadcasted_iota(jnp.int32, (cap, dests), 0)
    live = slot < counts_ref[...]
    items = [rows_ref[...].astype(F32)]
    items += [x.astype(F32) for x in split_three(values_ref[...])]
    items += [x.astype(F32) for x in split_three(jnp.where(live, precision_ref[...], 0.0))]
    items += [jnp.zeros((cap, dests), F32)]
    stacked = [x[c : c + 1] for c in range(cap) for x in items]
    stacked.append(jnp.zeros((out_ref.shape[3] - len(stacked), dests), F32))
    meta = jnp.concatenate(stacked, axis=0).T
    fp = fp_ref[...].astype(F32)
    fp = jnp.concatenate([fp, jnp.zeros_like(fp)], axis=1)
    stride = fp.shape[1]
    place = lax.broadcasted_iota(jnp.int32, fp.shape, 1)
    full_ref[...] = jnp.where(place == cap, meta[:, None, :], fp).reshape(full_ref.shape)
    inner, room, outer = out_ref.shape[:3]
    for i in range(inner):
        for r in range(room):
            out_ref[i, r] = full_ref[pl.ds(stride * i + r, outer, stride=stride * inner), :].astype(BF16)


def turn_body(in_ref, out_ref, rows_ref):
    inner, room, outer, columns = in_ref.shape
    wide = out_ref.shape[1]
    for i in range(inner):
        for r in range(room):
            rows_ref[pl.ds(room * i + r, outer, stride=wide), :] = in_ref[i, r].astype(F32)
    for r in range(inner * room, wide):
        rows_ref[pl.ds(r, outer, stride=wide), :] = jnp.zeros((outer, columns), F32)
    out_ref[...] = rows_ref[...].reshape(out_ref.shape).astype(BF16)


def first_body(fp_ref, counts_ref, rows_ref, values_ref, precision_ref, ens_ref, static_ref, e_ref, n_ref, out_ref, own_ref, full_ref):
    edges_body(ens_ref, static_ref, e_ref, n_ref, own_ref)
    message_body(fp_ref, counts_ref, rows_ref, values_ref, precision_ref, out_ref, full_ref)


def inner_increment_body(latitudes, scale, share, ens_ref, static_ref, sigma_ref, e_ref, n_ref, pert_ref, out_ref):
    members, slots = pert_ref.shape[:2]
    rows, columns = e_ref.shape
    edge = at_edge(lanes_of(e_ref.shape), columns)
    e, n = e_ref[...], closed(n_ref[...], latitudes)
    total = [jnp.zeros(e_ref.shape, F32) for _ in range(slots)]
    for m in range(members):
        u = smooth(ens_ref[m], e, n)
        for t in range(slots):
            total[t] = total[t] + pert_ref[m, t].astype(F32) * u
    static = (share * sigma_ref[...]) * smooth(static_ref[...], e, n)
    for t in range(slots):
        out_ref[t * rows : (t + 1) * rows, :] = jnp.where(edge, 0.0, scale * total[t] + static)


def outer_increment_body(
    latitudes, scale, share, inner_ref, own_ref, west_ref, east_ref, sigma_ref, e_ref, n_ref, pert_ref, out_ref, e_out, n_out
):
    members, slots = pert_ref.shape[:2]
    rows, columns = e_ref.shape
    fields = members + 1
    lane = lanes_of(e_ref.shape)
    own, from_west, from_east = own_ref[...], west_ref[...], east_ref[...]

    def coefficient(x, west, west_at, east, east_at):
        first = own_edges(x, EDGE, WIDE // 2 - EDGE, lane, jnp.zeros(x.shape, F32))
        first = jnp.where(lane < EDGE, turn(west, -west_at), first)
        ends = WIDE - EDGE
        first = jnp.where(between(lane, ends, WIDE), turn(east, ends - east_at), first)
        return repeated(first, fields, lane)

    e_at, n_at = WIDE * fields, WIDE * (fields + 1)
    e = coefficient(e_ref[...], from_west, e_at + WIDE - 2 * EDGE, from_east, e_at + EDGE)
    n = coefficient(n_ref[...], from_west, n_at + EDGE, from_east, n_at)
    n = closed(n, latitudes)
    e_out[...] = e
    n_out[...] = n
    packed = smooth(with_neighbours(own, from_west, from_east, fields, lane), e, n)
    total = [jnp.zeros(e_ref.shape, F32) for _ in range(slots)]
    for m in range(members):
        u = place_edges(packed, m, lane)
        for t in range(slots):
            total[t] = total[t] + pert_ref[m, t].astype(F32) * u
    static = (share * sigma_ref[...]) * place_edges(packed, members, lane)
    edge = at_edge(lane, columns)
    table = []
    for t in range(slots):
        table.append(jnp.where(edge, scale * total[t] + static, inner_ref[t * rows : (t + 1) * rows, :]))
    encode(jnp.concatenate(table, axis=0), out_ref)


def observe_body(cap, wide, parts_ref, seen_ref, out_ref):
    table = decode(parts_ref, 0, parts_ref.shape[1] - TAIL)
    rows, columns = table.shape
    high, low = split_two(table)
    seen = seen_ref[...]
    count = seen.shape[0]
    group = 8
    eye_shape = (group * cap, columns)
    eye = (
        lax.broadcasted_iota(jnp.int32, eye_shape, 0) == lax.broadcasted_iota(jnp.int32, eye_shape, 1)
    ).astype(F32).astype(BF16)
    contract = (((1,), (1,)), ((), ()))
    got = lax.dot_general(high, seen, contract, preferred_element_type=F32)
    got = got + lax.dot_general(low, seen, contract, preferred_element_type=F32)
    meta = lax.dot_general(eye, seen, contract, preferred_element_type=F32)
    at = lax.broadcasted_iota(jnp.int32, (group, count), 1) % wide
    place = jnp.where(at < RUN * (cap + 1), at % (cap + 1), cap)
    facts = jnp.zeros((group, count), F32)
    for c in range(cap):
        part = pltpu.roll(meta[c * group : (c + 1) * group], count - (cap - c), 1)
        facts = jnp.where(place == c, part, facts)
    row_of = jnp.where(place[:1] < cap, facts[0:1], -1.0).astype(jnp.int32)
    value = (facts[1:2] + facts[2:3]) + facts[3:4]
    precision = (facts[4:5] + facts[5:6]) + facts[6:7]
    hit = lax.broadcasted_iota(jnp.int32, (rows, count), 0) == row_of
    model = jnp.sum(jnp.where(hit, got, 0.0), axis=0, keepdims=True)
    residual = precision * (model - value)
    out = None
    for piece in split_two(residual):
        spread = jnp.where(hit, piece.astype(F32), 0.0).astype(BF16)
        term = jnp.dot(spread, seen, preferred_element_type=F32)
        out = term if out is None else out + term
    encode(out, out_ref)


def source_body(scale, parts_ref, pert_ref, sigma_ref, out_ref, packed_ref):
    members, slots, rows = pert_ref.shape[:3]
    gradient = []
    for t in range(slots):
        gradient.append(decode(parts_ref, t * rows, (t + 1) * rows))
    fields = []
    for m in range(members):
        u = pert_ref[m, 0].astype(F32) * gradient[0]
        for t in range(1, slots):
            u = u + pert_ref[m, t].astype(F32) * gradient[t]
        u = scale * u
        out_ref[m] = u
        fields.append(u)
    u = gradient[0]
    for t in range(1, slots):
        u = u + gradient[t]
    u = sigma_ref[...] * u
    out_ref[members] = u
    packed_ref[...] = pack_fields(fields + [u])


def inner_result_body(latitudes, source_ref, ens_ref, static_ref, e_ref, n_ref, out_ref):
    members = ens_ref.shape[0]
    e, n = e_ref[...], closed(n_ref[...], latitudes)
    for f in range(members + 1):
        out_ref[f] = smooth(source_ref[f], e, n) + (ens_ref[f] if f < members else static_ref[...])


def outer_result_body(inner_ref, own_ref, west_ref, east_ref, controls_ref, e_ref, n_ref, ens_out, static_out):
    members, _, columns = ens_out.shape
    lane = lanes_of(own_ref.shape)
    edge = at_edge(lane, columns)
    packed = with_neighbours(own_ref[...], west_ref[...], east_ref[...], members + 1, lane)
    packed = smooth(packed, e_ref[...], n_ref[...]) + controls_ref[...]
    for f in range(members + 1):
        u = jnp.where(edge, place_edges(packed, f, lane), inner_ref[f])
        if f < members:
            ens_out[f] = u
        else:
            static_out[...] = u


def on_device(
    control_ens,
    control_static,
    static_sigma,
    east_coef,
    north_coef,
    perturbations,
    obs_counts,
    obs_rows,
    footprints,
    obs_values,
    obs_precision,
):
    members, levels, latitudes, columns = control_ens.shape
    slots = perturbations.shape[1]
    rows = levels * latitudes
    table_rows = slots * rows
    groups = lax.axis_size("mem")
    scale = 1.0 / math.sqrt(members * groups - 1)
    ens = control_ens.reshape(members, rows, columns)
    static = control_static.reshape(rows, columns)
    sigma = static_sigma.reshape(rows, columns)
    e = east_coef.reshape(rows, columns)
    n = north_coef.reshape(rows, columns)
    pert = perturbations.reshape(members, slots, rows, columns)
    tiles, cap = obs_rows.shape[2:]

    field = shape((rows, columns))

    room = cap + 1
    wide = -(-RUN * room // 8) * 8
    message, own = call(
        first_body,
        (shape((RUN, room, tiles // RUN, columns), BF16), field),
        1e6,
        1e6,
        footprints[0, 0],
        obs_counts[0],
        obs_rows[0, 0].T,
        obs_values[0, 0].T,
        obs_precision[0, 0].T,
        ens,
        static,
        e,
        n,
        spec=BLOCKS,
        limit=60,
        scratch=[pltpu.VMEM((tiles * 2 * cap, columns), F32)],
    )
    west, east = from_neighbours(own, "tile")
    turned, seen = spread(message, "tile", wide)
    late, _ = lax.optimization_barrier((static, turned))

    share = 1.0 / groups
    coded = shape((table_rows + TAIL, columns), jnp.int16)
    inner = call(
        lambda *refs: inner_increment_body(latitudes, scale, share, *refs),
        shape((table_rows, columns)),
        BESIDE,
        4e6,
        ens,
        late,
        sigma,
        e,
        n,
        pert,
    )
    partial, e_packed, n_packed = call(
        lambda *refs: outer_increment_body(latitudes, scale, share, *refs),
        (coded, field, field),
        1e7,
        4e6,
        inner,
        own,
        west,
        east,
        sigma,
        e,
        n,
        pert,
    )
    parts = lax.all_gather(partial, "mem")
    partial_grad = call(
        lambda *refs: observe_body(cap, wide, *refs),
        coded,
        3e8,
        4e6,
        parts,
        seen.reshape(-1, columns),
    )
    grad_parts = lax.all_gather(partial_grad, "mem")
    source, own_source = call(
        lambda *refs: source_body(scale, *refs),
        (shape((members + 1, rows, columns)), field),
        1e7,
        2e6,
        grad_parts,
        pert,
        sigma,
    )
    west, east = from_neighbours(own_source, "tile")
    inner = call(
        lambda *refs: inner_result_body(latitudes, *refs),
        shape(source.shape),
        BESIDE,
        4e6,
        source,
        ens,
        static,
        e,
        n,
    )
    ens_out, static_out = call(
        outer_result_body,
        (shape(ens.shape), field),
        1e7,
        2e6,
        inner,
        own_source,
        west,
        east,
        own,
        e_packed,
        n_packed,
    )
    return ens_out.reshape(control_ens.shape), static_out.reshape(control_static.shape)


def solution(mesh):
    placed = (
        P("mem", None, None, "tile"),
        P(None, None, "tile"),
        P(None, None, "tile"),
        P(None, None, "tile"),
        P(None, None, "tile"),
        P("mem", None, None, None, "tile"),
        P("mem", "tile", None),
        P("mem", "tile", None, None),
        P("mem", "tile", None, None, None),
        P("mem", "tile", None, None),
        P("mem", "tile", None, None),
    )
    return jax.shard_map(
        on_device,
        mesh=mesh,
        in_specs=placed,
        out_specs=(P("mem", None, None, "tile"), P(None, None, "tile")),
        check_vma=False,
    )
```

```python
import functools
import math

import jax
import jax.numpy as jnp
from jax import lax
from jax.experimental import pallas as pl
from jax.experimental.pallas import tpu as pltpu
from jax.sharding import PartitionSpec as P

SWEEPS = 2
F32 = jnp.float32
BF16 = jnp.bfloat16
BESIDE = 1e9
RUN = 4
TURN = 2e10
VMEM = pl.BlockSpec(memory_space=pltpu.VMEM)
SCALAR = pl.BlockSpec(memory_space=pltpu.SMEM)
BLOCKS = pl.BlockSpec()


def call(body, out, flops, traffic, *operands, spec=VMEM, specs=None, limit=32, scratch=()):
    return pl.pallas_call(
        body,
        out_shape=out,
        in_specs=specs or [spec] * len(operands),
        out_specs=jax.tree.map(lambda _: VMEM, out),
        scratch_shapes=scratch,
        cost_estimate=pl.CostEstimate(flops=int(flops), bytes_accessed=int(traffic), transcendentals=0),
        compiler_params=pltpu.CompilerParams(vmem_limit_bytes=limit * 1024 * 1024),
    )(*operands)


def shape(dims, kind=F32):
    return jax.ShapeDtypeStruct(dims, kind)


def from_neighbours(x, axis):
    count = lax.axis_size(axis)
    swaps = []
    for start in (1, 0):
        pairs = [(i % count, (i + 1) % count) for i in range(start, count + start, 2)]
        swaps.append(lax.ppermute(x, axis, pairs + [(j, i) for i, j in pairs]))
    odd = lax.axis_index(axis) % 2 == 1
    return jnp.where(odd, swaps[1], swaps[0]), jnp.where(odd, swaps[0], swaps[1])


def runs_of(axis):
    outer = lax.axis_size(axis) // RUN
    runs = [[o * RUN + i for i in range(RUN)] for o in range(outer)]
    return runs, [list(tiles) for tiles in zip(*runs)]


def between_runs(x, axis):
    count = lax.axis_size(axis)
    pairs = [((i + RUN - 1) % count, (i + RUN) % count) for i in range(0, count, RUN)]
    return lax.ppermute(x, axis, pairs + [(j, i) for i, j in pairs])


def split_two(x):
    high = x.astype(BF16)
    return high, (x - high.astype(F32)).astype(BF16)


def split_three(x):
    high = x.astype(BF16)
    rest = x - high.astype(F32)
    mid = rest.astype(BF16)
    return high, mid, (rest - mid.astype(F32)).astype(BF16)


STEPS = 256
LARGEST = 32600.0
TAIL = 16


def scale_of(steps):
    return jnp.exp2(steps * (1.0 / STEPS))


def encode(table, out_ref):
    rows, columns = table.shape
    most = jnp.max(jnp.abs(table), axis=0, keepdims=True)
    steps = jnp.ceil(jnp.log2(jnp.maximum(most, 1e-30)) * STEPS)
    coded = jnp.round(table * (LARGEST / scale_of(steps)))
    out_ref[0:rows, :] = coded.astype(jnp.int32).astype(jnp.int16)
    tail = jnp.broadcast_to(steps, (TAIL, columns))
    out_ref[rows : rows + TAIL, :] = tail.astype(jnp.int32).astype(jnp.int16)


def decode(parts_ref, low, high):
    rows = parts_ref.shape[1] - TAIL
    total = None
    for k in range(parts_ref.shape[0]):
        steps = parts_ref[k, rows : rows + TAIL, :].astype(jnp.int32).astype(F32)[0:1]
        unit = scale_of(steps) * (1.0 / LARGEST)
        part = parts_ref[k, low:high, :].astype(jnp.int32).astype(F32) * unit
        total = part if total is None else total + part
    return total


WIDE = 12
EDGE = 2


def lanes_of(dims):
    return lax.broadcasted_iota(jnp.int32, dims, 1)


def turn(x, by):
    by = by % x.shape[1]
    return pltpu.roll(x, by, 1) if by else x


def between(lane, low, high):
    return (lane >= low) & (lane < high)


def own_edges(x, start, keep, lane, packed):
    columns = x.shape[1]
    packed = jnp.where(between(lane, start, start + keep), turn(x, start), packed)
    end = start + 2 * keep
    return jnp.where(between(lane, start + keep, end), turn(x, end - columns), packed)


def pack_fields(fields):
    packed = jnp.zeros(fields[0].shape, F32)
    lane = lanes_of(packed.shape)
    for f, u in enumerate(fields):
        packed = own_edges(u, WIDE * f + EDGE, WIDE // 2 - EDGE, lane, packed)
    return packed


def place_edges(packed, f, lane):
    columns = packed.shape[1]
    start = WIDE * f + EDGE
    left = turn(packed, -start)
    right = turn(packed, columns - (WIDE * (f + 1) - EDGE))
    return jnp.where(lane < EDGE, left, right)


def at_edge(lane, columns):
    return (lane < EDGE) | (lane >= columns - EDGE)


def diffuse(u, e, n):
    rows = u.shape[0]
    flux = e * (turn(u, -1) - u)
    up = n * (pltpu.roll(u, rows - 1, 0) - u)
    return u + ((flux - turn(flux, 1)) + (up - pltpu.roll(up, 1, 0)))


def smooth(u, e, n):
    for _ in range(SWEEPS):
        u = diffuse(u, e, n)
    return u


def closed(n, latitudes):
    row = lax.broadcasted_iota(jnp.int32, n.shape, 0)
    return jnp.where((row & (latitudes - 1)) == latitudes - 1, 0.0, n)


def with_neighbours(own, from_west, from_east, fields, lane):
    at = lane % WIDE
    west = (at < EDGE) & (lane < WIDE * fields)
    east = (at >= WIDE - EDGE) & (lane < WIDE * fields)
    out = jnp.where(west, turn(from_west, 2 * EDGE - WIDE), own)
    return jnp.where(east, turn(from_east, WIDE - 2 * EDGE), out)


def repeated(first, count, lane):
    out, have = first, 1
    while have < count:
        out = jnp.where(lane < WIDE * have, out, turn(out, WIDE * have))
        have *= 2
    return out


def edges_body(ens_ref, static_ref, e_ref, n_ref, out_ref):
    members = ens_ref.shape[0]
    packed = pack_fields([ens_ref[m] for m in range(members)] + [static_ref[...], e_ref[...]])
    start = WIDE * (members + 2)
    out_ref[...] = own_edges(n_ref[...], start, EDGE, lanes_of(packed.shape), packed)


def message_body(fp_ref, counts_ref, rows_ref, values_ref, precision_ref, out_ref, full_ref):
    cap, dests = rows_ref.shape
    slot = lax.broadcasted_iota(jnp.int32, (cap, dests), 0)
    live = slot < counts_ref[...]
    items = [rows_ref[...].astype(F32)]
    items += [x.astype(F32) for x in split_three(values_ref[...])]
    items += [x.astype(F32) for x in split_three(jnp.where(live, precision_ref[...], 0.0))]
    items += [jnp.zeros((cap, dests), F32)]
    stacked = [x[c : c + 1] for c in range(cap) for x in items]
    stacked.append(jnp.zeros((out_ref.shape[2] - len(stacked), dests), F32))
    meta = jnp.concatenate(stacked, axis=0).T
    fp = fp_ref[...].astype(F32)
    fp = jnp.concatenate([fp, jnp.zeros_like(fp)], axis=1)
    stride = fp.shape[1]
    place = lax.broadcasted_iota(jnp.int32, fp.shape, 1)
    full_ref[...] = jnp.where(place == cap, meta[:, None, :], fp).reshape(full_ref.shape)
    inner = out_ref.shape[0]
    outer = dests // inner
    for i in range(inner):
        for r in range(cap + 1):
            part = full_ref[pl.ds(stride * i + r, outer, stride=stride * inner), :]
            out_ref[i, r * outer : (r + 1) * outer, :] = part.astype(BF16)


def turn_body(room, x_ref, in_ref, out_ref, west_ref, east_ref, rows_ref):
    inner, columns = in_ref.shape[0], in_ref.shape[2]
    outer, wide = out_ref.shape[:2]
    for i in range(inner):
        for r in range(room):
            part = in_ref[i, r * outer : (r + 1) * outer, :].astype(F32)
            rows_ref[pl.ds(room * i + r, outer, stride=wide), :] = part
    for r in range(inner * room, wide):
        rows_ref[pl.ds(r, outer, stride=wide), :] = jnp.zeros((outer, columns), F32)
    out_ref[...] = rows_ref[...].reshape(out_ref.shape).astype(BF16)
    rows = west_ref.shape[0]
    high = room * outer
    x = x_ref[0]
    for at, ref in ((x - 1, west_ref), (x + 1, east_ref)):
        at = jnp.clip(at, 0, inner - 1)
        edges = in_ref[at, high : high + rows, :].astype(F32)
        ref[...] = edges + in_ref[at, high + rows : high + 2 * rows, :].astype(F32)


def first_body(fp_ref, counts_ref, rows_ref, values_ref, precision_ref, ens_ref, static_ref, e_ref, n_ref, out_ref, own_ref, full_ref):
    edges_body(ens_ref, static_ref, e_ref, n_ref, own_ref)
    message_body(fp_ref, counts_ref, rows_ref, values_ref, precision_ref, out_ref, full_ref)
    rows = own_ref.shape[0]
    at = out_ref.shape[1] - 2 * rows
    for piece in split_two(own_ref[...]):
        for i in range(out_ref.shape[0]):
            out_ref[i, at : at + rows, :] = piece
        at += rows


def inner_increment_body(latitudes, scale, share, ens_ref, static_ref, sigma_ref, e_ref, n_ref, pert_ref, out_ref):
    members, slots = pert_ref.shape[:2]
    rows, columns = e_ref.shape
    edge = at_edge(lanes_of(e_ref.shape), columns)
    e, n = e_ref[...], closed(n_ref[...], latitudes)
    total = [jnp.zeros(e_ref.shape, F32) for _ in range(slots)]
    for m in range(members):
        u = smooth(ens_ref[m], e, n)
        for t in range(slots):
            total[t] = total[t] + pert_ref[m, t].astype(F32) * u
    static = (share * sigma_ref[...]) * smooth(static_ref[...], e, n)
    for t in range(slots):
        out_ref[t * rows : (t + 1) * rows, :] = jnp.where(edge, 0.0, scale * total[t] + static)


def outer_increment_body(
    latitudes, scale, share, x_ref, inner_ref, own_ref, far_ref, west_ref, east_ref, sigma_ref, e_ref, n_ref, pert_ref, out_ref, e_out, n_out
):
    members, slots = pert_ref.shape[:2]
    rows, columns = e_ref.shape
    fields = members + 1
    lane = lanes_of(e_ref.shape)
    own, far, x = own_ref[...], far_ref[...], x_ref[0]
    from_west = jnp.where(x == 0, far, west_ref[...])
    from_east = jnp.where(x == RUN - 1, far, east_ref[...])

    def coefficient(x, west, west_at, east, east_at):
        first = own_edges(x, EDGE, WIDE // 2 - EDGE, lane, jnp.zeros(x.shape, F32))
        first = jnp.where(lane < EDGE, turn(west, -west_at), first)
        ends = WIDE - EDGE
        first = jnp.where(between(lane, ends, WIDE), turn(east, ends - east_at), first)
        return repeated(first, fields, lane)

    e_at, n_at = WIDE * fields, WIDE * (fields + 1)
    e = coefficient(e_ref[...], from_west, e_at + WIDE - 2 * EDGE, from_east, e_at + EDGE)
    n = coefficient(n_ref[...], from_west, n_at + EDGE, from_east, n_at)
    n = closed(n, latitudes)
    e_out[...] = e
    n_out[...] = n
    packed = smooth(with_neighbours(own, from_west, from_east, fields, lane), e, n)
    total = [jnp.zeros(e_ref.shape, F32) for _ in range(slots)]
    for m in range(members):
        u = place_edges(packed, m, lane)
        for t in range(slots):
            total[t] = total[t] + pert_ref[m, t].astype(F32) * u
    static = (share * sigma_ref[...]) * place_edges(packed, members, lane)
    edge = at_edge(lane, columns)
    table = []
    for t in range(slots):
        table.append(jnp.where(edge, scale * total[t] + static, inner_ref[t * rows : (t + 1) * rows, :]))
    encode(jnp.concatenate(table, axis=0), out_ref)


def observe_body(cap, wide, parts_ref, seen_ref, out_ref):
    table = decode(parts_ref, 0, parts_ref.shape[1] - TAIL)
    rows, columns = table.shape
    high, low = split_two(table)
    seen = seen_ref[...]
    count = seen.shape[0]
    group = 8
    eye_shape = (group * cap, columns)
    eye = (
        lax.broadcasted_iota(jnp.int32, eye_shape, 0) == lax.broadcasted_iota(jnp.int32, eye_shape, 1)
    ).astype(F32).astype(BF16)
    contract = (((1,), (1,)), ((), ()))
    got = lax.dot_general(high, seen, contract, preferred_element_type=F32)
    got = got + lax.dot_general(low, seen, contract, preferred_element_type=F32)
    meta = lax.dot_general(eye, seen, contract, preferred_element_type=F32)
    at = lax.broadcasted_iota(jnp.int32, (group, count), 1) % wide
    place = jnp.where(at < RUN * (cap + 1), at % (cap + 1), cap)
    facts = jnp.zeros((group, count), F32)
    for c in range(cap):
        part = pltpu.roll(meta[c * group : (c + 1) * group], count - (cap - c), 1)
        facts = jnp.where(place == c, part, facts)
    row_of = jnp.where(place[:1] < cap, facts[0:1], -1.0).astype(jnp.int32)
    value = (facts[1:2] + facts[2:3]) + facts[3:4]
    precision = (facts[4:5] + facts[5:6]) + facts[6:7]
    hit = lax.broadcasted_iota(jnp.int32, (rows, count), 0) == row_of
    model = jnp.sum(jnp.where(hit, got, 0.0), axis=0, keepdims=True)
    residual = precision * (model - value)
    out = None
    for piece in split_two(residual):
        spread = jnp.where(hit, piece.astype(F32), 0.0).astype(BF16)
        term = jnp.dot(spread, seen, preferred_element_type=F32)
        out = term if out is None else out + term
    encode(out, out_ref)


def source_body(scale, parts_ref, pert_ref, sigma_ref, out_ref, packed_ref):
    members, slots, rows = pert_ref.shape[:3]
    gradient = []
    for t in range(slots):
        gradient.append(decode(parts_ref, t * rows, (t + 1) * rows))
    fields = []
    for m in range(members):
        u = pert_ref[m, 0].astype(F32) * gradient[0]
        for t in range(1, slots):
            u = u + pert_ref[m, t].astype(F32) * gradient[t]
        u = scale * u
        out_ref[m] = u
        fields.append(u)
    u = gradient[0]
    for t in range(1, slots):
        u = u + gradient[t]
    u = sigma_ref[...] * u
    out_ref[members] = u
    packed_ref[...] = pack_fields(fields + [u])


def inner_result_body(latitudes, source_ref, ens_ref, static_ref, e_ref, n_ref, out_ref):
    members = ens_ref.shape[0]
    e, n = e_ref[...], closed(n_ref[...], latitudes)
    for f in range(members + 1):
        out_ref[f] = smooth(source_ref[f], e, n) + (ens_ref[f] if f < members else static_ref[...])


def outer_result_body(inner_ref, own_ref, west_ref, east_ref, controls_ref, e_ref, n_ref, ens_out, static_out):
    members, _, columns = ens_out.shape
    lane = lanes_of(own_ref.shape)
    edge = at_edge(lane, columns)
    packed = with_neighbours(own_ref[...], west_ref[...], east_ref[...], members + 1, lane)
    packed = smooth(packed, e_ref[...], n_ref[...]) + controls_ref[...]
    for f in range(members + 1):
        u = jnp.where(edge, place_edges(packed, f, lane), inner_ref[f])
        if f < members:
            ens_out[f] = u
        else:
            static_out[...] = u


def on_device(
    control_ens,
    control_static,
    static_sigma,
    east_coef,
    north_coef,
    perturbations,
    obs_counts,
    obs_rows,
    footprints,
    obs_values,
    obs_precision,
):
    members, levels, latitudes, columns = control_ens.shape
    slots = perturbations.shape[1]
    rows = levels * latitudes
    table_rows = slots * rows
    groups = lax.axis_size("mem")
    scale = 1.0 / math.sqrt(members * groups - 1)
    ens = control_ens.reshape(members, rows, columns)
    static = control_static.reshape(rows, columns)
    sigma = static_sigma.reshape(rows, columns)
    e = east_coef.reshape(rows, columns)
    n = north_coef.reshape(rows, columns)
    pert = perturbations.reshape(members, slots, rows, columns)
    tiles, cap = obs_rows.shape[2:]

    field = shape((rows, columns))

    room = cap + 1
    wide = -(-RUN * room // 8) * 8
    runs, across = runs_of("tile")
    outer = len(runs)
    message, own = call(
        first_body,
        (shape((RUN, room * outer + 2 * rows, columns), BF16), field),
        1e6,
        1e6,
        footprints[0, 0],
        obs_counts[0],
        obs_rows[0, 0].T,
        obs_values[0, 0].T,
        obs_precision[0, 0].T,
        ens,
        static,
        e,
        n,
        spec=BLOCKS,
        limit=60,
        scratch=[pltpu.VMEM((tiles * 2 * cap, columns), F32)],
    )
    message = lax.all_to_all(message, "tile", 0, 0, axis_index_groups=runs, tiled=True)
    far = between_runs(own, "tile")
    x = (lax.axis_index("tile") % RUN).reshape(1)
    message, west, east = call(
        functools.partial(turn_body, room),
        (shape((outer, wide, columns), BF16), field, field),
        TURN,
        1e6,
        x,
        message,
        specs=[SCALAR, VMEM],
        scratch=[pltpu.VMEM((outer * wide, columns), F32)],
    )
    seen = lax.all_to_all(message, "tile", 0, 0, axis_index_groups=across, tiled=True)
    late, _ = lax.optimization_barrier((static, message))

    share = 1.0 / groups
    coded = shape((table_rows + TAIL, columns), jnp.int16)
    inner = call(
        lambda *refs: inner_increment_body(latitudes, scale, share, *refs),
        shape((table_rows, columns)),
        BESIDE,
        4e6,
        ens,
        late,
        sigma,
        e,
        n,
        pert,
    )
    partial, e_packed, n_packed = call(
        lambda *refs: outer_increment_body(latitudes, scale, share, *refs),
        (coded, field, field),
        4e9,
        4e6,
        x,
        inner,
        own,
        far,
        west,
        east,
        sigma,
        e,
        n,
        pert,
        specs=[SCALAR] + [VMEM] * 9,
    )
    parts = lax.all_gather(partial, "mem")
    partial_grad = call(
        lambda *refs: observe_body(cap, wide, *refs),
        coded,
        3e8,
        4e6,
        parts,
        seen.reshape(-1, columns),
    )
    grad_parts = lax.all_gather(partial_grad, "mem")
    source, own_source = call(
        lambda *refs: source_body(scale, *refs),
        (shape((members + 1, rows, columns)), field),
        1e7,
        2e6,
        grad_parts,
        pert,
        sigma,
    )
    west, east = from_neighbours(own_source, "tile")
    inner = call(
        lambda *refs: inner_result_body(latitudes, *refs),
        shape(source.shape),
        BESIDE,
        4e6,
        source,
        ens,
        static,
        e,
        n,
    )
    ens_out, static_out = call(
        outer_result_body,
        (shape(ens.shape), field),
        1e7,
        2e6,
        inner,
        own_source,
        west,
        east,
        own,
        e_packed,
        n_packed,
    )
    return ens_out.reshape(control_ens.shape), static_out.reshape(control_static.shape)


def solution(mesh):
    placed = (
        P("mem", None, None, "tile"),
        P(None, None, "tile"),
        P(None, None, "tile"),
        P(None, None, "tile"),
        P(None, None, "tile"),
        P("mem", None, None, None, "tile"),
        P("mem", "tile", None),
        P("mem", "tile", None, None),
        P("mem", "tile", None, None, None),
        P("mem", "tile", None, None),
        P("mem", "tile", None, None),
    )
    return jax.shard_map(
        on_device,
        mesh=mesh,
        in_specs=placed,
        out_specs=(P("mem", None, None, "tile"), P(None, None, "tile")),
        check_vma=False,
    )
```

```python
import functools
import math

import jax
import jax.numpy as jnp
from jax import lax
from jax.experimental import pallas as pl
from jax.experimental.pallas import tpu as pltpu
from jax.sharding import PartitionSpec as P

SWEEPS = 2
F32 = jnp.float32
BF16 = jnp.bfloat16
BESIDE = 1e9
RUN = 4
TURN = 2e10
VMEM = pl.BlockSpec(memory_space=pltpu.VMEM)
SCALAR = pl.BlockSpec(memory_space=pltpu.SMEM)
BLOCKS = pl.BlockSpec()


def call(body, out, flops, traffic, *operands, spec=VMEM, specs=None, limit=32, scratch=()):
    return pl.pallas_call(
        body,
        out_shape=out,
        in_specs=specs or [spec] * len(operands),
        out_specs=jax.tree.map(lambda _: VMEM, out),
        scratch_shapes=scratch,
        cost_estimate=pl.CostEstimate(flops=int(flops), bytes_accessed=int(traffic), transcendentals=0),
        compiler_params=pltpu.CompilerParams(vmem_limit_bytes=limit * 1024 * 1024),
    )(*operands)


def shape(dims, kind=F32):
    return jax.ShapeDtypeStruct(dims, kind)


def from_neighbours(x, axis):
    count = lax.axis_size(axis)
    swaps = []
    for start in (1, 0):
        pairs = [(i % count, (i + 1) % count) for i in range(start, count + start, 2)]
        swaps.append(lax.ppermute(x, axis, pairs + [(j, i) for i, j in pairs]))
    odd = lax.axis_index(axis) % 2 == 1
    return jnp.where(odd, swaps[1], swaps[0]), jnp.where(odd, swaps[0], swaps[1])


def runs_of(axis):
    outer = lax.axis_size(axis) // RUN
    runs = [[o * RUN + i for i in range(RUN)] for o in range(outer)]
    return runs, [list(tiles) for tiles in zip(*runs)]


def between_runs(x, axis):
    count = lax.axis_size(axis)
    pairs = [((i + RUN - 1) % count, (i + RUN) % count) for i in range(0, count, RUN)]
    return lax.ppermute(x, axis, pairs + [(j, i) for i, j in pairs])


def split_two(x):
    high = x.astype(BF16)
    return high, (x - high.astype(F32)).astype(BF16)


def split_three(x):
    high = x.astype(BF16)
    rest = x - high.astype(F32)
    mid = rest.astype(BF16)
    return high, mid, (rest - mid.astype(F32)).astype(BF16)


STEPS = 256
LARGEST = 32600.0
TAIL = 16


def scale_of(steps):
    return jnp.exp2(steps * (1.0 / STEPS))


def encode(table, out_ref):
    rows, columns = table.shape
    most = jnp.max(jnp.abs(table), axis=0, keepdims=True)
    steps = jnp.ceil(jnp.log2(jnp.maximum(most, 1e-30)) * STEPS)
    coded = jnp.round(table * (LARGEST / scale_of(steps)))
    out_ref[0:rows, :] = coded.astype(jnp.int32).astype(jnp.int16)
    tail = jnp.broadcast_to(steps, (TAIL, columns))
    out_ref[rows : rows + TAIL, :] = tail.astype(jnp.int32).astype(jnp.int16)


def decode(parts_ref, low, high):
    rows = parts_ref.shape[1] - TAIL
    total = None
    for k in range(parts_ref.shape[0]):
        steps = parts_ref[k, rows : rows + TAIL, :].astype(jnp.int32).astype(F32)[0:1]
        unit = scale_of(steps) * (1.0 / LARGEST)
        part = parts_ref[k, low:high, :].astype(jnp.int32).astype(F32) * unit
        total = part if total is None else total + part
    return total


WIDE = 12
EDGE = 2


def lanes_of(dims):
    return lax.broadcasted_iota(jnp.int32, dims, 1)


def turn(x, by):
    by = by % x.shape[1]
    return pltpu.roll(x, by, 1) if by else x


def between(lane, low, high):
    return (lane >= low) & (lane < high)


def own_edges(x, start, keep, lane, packed):
    columns = x.shape[1]
    packed = jnp.where(between(lane, start, start + keep), turn(x, start), packed)
    end = start + 2 * keep
    return jnp.where(between(lane, start + keep, end), turn(x, end - columns), packed)


def pack_fields(fields):
    packed = jnp.zeros(fields[0].shape, F32)
    lane = lanes_of(packed.shape)
    for f, u in enumerate(fields):
        packed = own_edges(u, WIDE * f + EDGE, WIDE // 2 - EDGE, lane, packed)
    return packed


def place_edges(packed, f, lane):
    columns = packed.shape[1]
    start = WIDE * f + EDGE
    left = turn(packed, -start)
    right = turn(packed, columns - (WIDE * (f + 1) - EDGE))
    return jnp.where(lane < EDGE, left, right)


def at_edge(lane, columns):
    return (lane < EDGE) | (lane >= columns - EDGE)


def diffuse(u, e, n):
    rows = u.shape[0]
    flux = e * (turn(u, -1) - u)
    up = n * (pltpu.roll(u, rows - 1, 0) - u)
    return u + ((flux - turn(flux, 1)) + (up - pltpu.roll(up, 1, 0)))


def smooth(u, e, n):
    for _ in range(SWEEPS):
        u = diffuse(u, e, n)
    return u


def closed(n, latitudes):
    row = lax.broadcasted_iota(jnp.int32, n.shape, 0)
    return jnp.where((row & (latitudes - 1)) == latitudes - 1, 0.0, n)


def with_neighbours(own, from_west, from_east, fields, lane):
    at = lane % WIDE
    west = (at < EDGE) & (lane < WIDE * fields)
    east = (at >= WIDE - EDGE) & (lane < WIDE * fields)
    out = jnp.where(west, turn(from_west, 2 * EDGE - WIDE), own)
    return jnp.where(east, turn(from_east, WIDE - 2 * EDGE), out)


def repeated(first, count, lane):
    out, have = first, 1
    while have < count:
        out = jnp.where(lane < WIDE * have, out, turn(out, WIDE * have))
        have *= 2
    return out


def edges_body(ens_ref, static_ref, e_ref, n_ref, out_ref):
    members = ens_ref.shape[0]
    packed = pack_fields([ens_ref[m] for m in range(members)] + [static_ref[...], e_ref[...]])
    start = WIDE * (members + 2)
    out_ref[...] = own_edges(n_ref[...], start, EDGE, lanes_of(packed.shape), packed)


def message_body(fp_ref, counts_ref, rows_ref, values_ref, precision_ref, out_ref, full_ref):
    cap, dests = rows_ref.shape
    slot = lax.broadcasted_iota(jnp.int32, (cap, dests), 0)
    live = slot < counts_ref[...]
    items = [rows_ref[...].astype(F32)]
    items += [x.astype(F32) for x in split_three(values_ref[...])]
    items += [x.astype(F32) for x in split_three(jnp.where(live, precision_ref[...], 0.0))]
    items += [jnp.zeros((cap, dests), F32)]
    stacked = [x[c : c + 1] for c in range(cap) for x in items]
    stacked.append(jnp.zeros((out_ref.shape[2] - len(stacked), dests), F32))
    meta = jnp.concatenate(stacked, axis=0).T
    fp = fp_ref[...].astype(F32)
    fp = jnp.concatenate([fp, jnp.zeros_like(fp)], axis=1)
    stride = fp.shape[1]
    place = lax.broadcasted_iota(jnp.int32, fp.shape, 1)
    full_ref[...] = jnp.where(place == cap, meta[:, None, :], fp).reshape(full_ref.shape)
    inner = out_ref.shape[0]
    outer = dests // inner
    for i in range(inner):
        for r in range(cap + 1):
            part = full_ref[pl.ds(stride * i + r, outer, stride=stride * inner), :]
            out_ref[i, r * outer : (r + 1) * outer, :] = part.astype(BF16)


def turn_body(room, x_ref, in_ref, out_ref, west_ref, east_ref, rows_ref):
    inner, columns = in_ref.shape[0], in_ref.shape[2]
    outer, wide = out_ref.shape[:2]
    for i in range(inner):
        for r in range(room):
            part = in_ref[i, r * outer : (r + 1) * outer, :].astype(F32)
            rows_ref[pl.ds(room * i + r, outer, stride=wide), :] = part
    for r in range(inner * room, wide):
        rows_ref[pl.ds(r, outer, stride=wide), :] = jnp.zeros((outer, columns), F32)
    out_ref[...] = rows_ref[...].reshape(out_ref.shape).astype(BF16)
    rows = west_ref.shape[0]
    high = room * outer
    x = x_ref[0]
    for at, ref in ((x - 1, west_ref), (x + 1, east_ref)):
        at = jnp.clip(at, 0, inner - 1)
        ref[...] = in_ref[at, high : high + rows, :].astype(F32)


def first_body(fp_ref, counts_ref, rows_ref, values_ref, precision_ref, ens_ref, static_ref, e_ref, n_ref, out_ref, own_ref, full_ref):
    edges_body(ens_ref, static_ref, e_ref, n_ref, own_ref)
    message_body(fp_ref, counts_ref, rows_ref, values_ref, precision_ref, out_ref, full_ref)
    rows = own_ref.shape[0]
    at = out_ref.shape[1] - rows
    for i in range(out_ref.shape[0]):
        out_ref[i, at : at + rows, :] = own_ref[...].astype(BF16)


def inner_increment_body(latitudes, scale, share, ens_ref, static_ref, sigma_ref, e_ref, n_ref, pert_ref, out_ref):
    members, slots = pert_ref.shape[:2]
    rows, columns = e_ref.shape
    edge = at_edge(lanes_of(e_ref.shape), columns)
    e, n = e_ref[...], closed(n_ref[...], latitudes)
    total = [jnp.zeros(e_ref.shape, F32) for _ in range(slots)]
    for m in range(members):
        u = smooth(ens_ref[m], e, n)
        for t in range(slots):
            total[t] = total[t] + pert_ref[m, t].astype(F32) * u
    static = (share * sigma_ref[...]) * smooth(static_ref[...], e, n)
    for t in range(slots):
        out_ref[t * rows : (t + 1) * rows, :] = jnp.where(edge, 0.0, scale * total[t] + static)


def outer_increment_body(
    latitudes, scale, share, x_ref, inner_ref, own_ref, far_ref, west_ref, east_ref, sigma_ref, e_ref, n_ref, pert_ref, out_ref, e_out, n_out
):
    members, slots = pert_ref.shape[:2]
    rows, columns = e_ref.shape
    fields = members + 1
    lane = lanes_of(e_ref.shape)
    own, far, x = own_ref[...], far_ref[...], x_ref[0]
    from_west = jnp.where(x == 0, far, west_ref[...])
    from_east = jnp.where(x == RUN - 1, far, east_ref[...])

    def coefficient(x, west, west_at, east, east_at):
        first = own_edges(x, EDGE, WIDE // 2 - EDGE, lane, jnp.zeros(x.shape, F32))
        first = jnp.where(lane < EDGE, turn(west, -west_at), first)
        ends = WIDE - EDGE
        first = jnp.where(between(lane, ends, WIDE), turn(east, ends - east_at), first)
        return repeated(first, fields, lane)

    e_at, n_at = WIDE * fields, WIDE * (fields + 1)
    e = coefficient(e_ref[...], from_west, e_at + WIDE - 2 * EDGE, from_east, e_at + EDGE)
    n = coefficient(n_ref[...], from_west, n_at + EDGE, from_east, n_at)
    n = closed(n, latitudes)
    e_out[...] = e
    n_out[...] = n
    packed = smooth(with_neighbours(own, from_west, from_east, fields, lane), e, n)
    total = [jnp.zeros(e_ref.shape, F32) for _ in range(slots)]
    for m in range(members):
        u = place_edges(packed, m, lane)
        for t in range(slots):
            total[t] = total[t] + pert_ref[m, t].astype(F32) * u
    static = (share * sigma_ref[...]) * place_edges(packed, members, lane)
    edge = at_edge(lane, columns)
    table = []
    for t in range(slots):
        table.append(jnp.where(edge, scale * total[t] + static, inner_ref[t * rows : (t + 1) * rows, :]))
    encode(jnp.concatenate(table, axis=0), out_ref)


def observe_body(cap, wide, parts_ref, seen_ref, out_ref):
    table = decode(parts_ref, 0, parts_ref.shape[1] - TAIL)
    rows, columns = table.shape
    high, low = split_two(table)
    seen = seen_ref[...]
    count = seen.shape[0]
    group = 8
    eye_shape = (group * cap, columns)
    eye = (
        lax.broadcasted_iota(jnp.int32, eye_shape, 0) == lax.broadcasted_iota(jnp.int32, eye_shape, 1)
    ).astype(F32).astype(BF16)
    contract = (((1,), (1,)), ((), ()))
    got = lax.dot_general(high, seen, contract, preferred_element_type=F32)
    got = got + lax.dot_general(low, seen, contract, preferred_element_type=F32)
    meta = lax.dot_general(eye, seen, contract, preferred_element_type=F32)
    at = lax.broadcasted_iota(jnp.int32, (group, count), 1) % wide
    place = jnp.where(at < RUN * (cap + 1), at % (cap + 1), cap)
    facts = jnp.zeros((group, count), F32)
    for c in range(cap):
        part = pltpu.roll(meta[c * group : (c + 1) * group], count - (cap - c), 1)
        facts = jnp.where(place == c, part, facts)
    row_of = jnp.where(place[:1] < cap, facts[0:1], -1.0).astype(jnp.int32)
    value = (facts[1:2] + facts[2:3]) + facts[3:4]
    precision = (facts[4:5] + facts[5:6]) + facts[6:7]
    hit = lax.broadcasted_iota(jnp.int32, (rows, count), 0) == row_of
    model = jnp.sum(jnp.where(hit, got, 0.0), axis=0, keepdims=True)
    residual = precision * (model - value)
    out = None
    for piece in split_two(residual):
        spread = jnp.where(hit, piece.astype(F32), 0.0).astype(BF16)
        term = jnp.dot(spread, seen, preferred_element_type=F32)
        out = term if out is None else out + term
    encode(out, out_ref)


def source_body(scale, parts_ref, pert_ref, sigma_ref, out_ref, packed_ref):
    members, slots, rows = pert_ref.shape[:3]
    gradient = []
    for t in range(slots):
        gradient.append(decode(parts_ref, t * rows, (t + 1) * rows))
    fields = []
    for m in range(members):
        u = pert_ref[m, 0].astype(F32) * gradient[0]
        for t in range(1, slots):
            u = u + pert_ref[m, t].astype(F32) * gradient[t]
        u = scale * u
        out_ref[m] = u
        fields.append(u)
    u = gradient[0]
    for t in range(1, slots):
        u = u + gradient[t]
    u = sigma_ref[...] * u
    out_ref[members] = u
    packed_ref[...] = pack_fields(fields + [u])


def inner_result_body(latitudes, source_ref, ens_ref, static_ref, e_ref, n_ref, out_ref):
    members = ens_ref.shape[0]
    e, n = e_ref[...], closed(n_ref[...], latitudes)
    for f in range(members + 1):
        out_ref[f] = smooth(source_ref[f], e, n) + (ens_ref[f] if f < members else static_ref[...])


def outer_result_body(inner_ref, own_ref, west_ref, east_ref, controls_ref, e_ref, n_ref, ens_out, static_out):
    members, _, columns = ens_out.shape
    lane = lanes_of(own_ref.shape)
    edge = at_edge(lane, columns)
    packed = with_neighbours(own_ref[...], west_ref[...].astype(F32), east_ref[...].astype(F32), members + 1, lane)
    packed = smooth(packed, e_ref[...], n_ref[...]) + controls_ref[...]
    for f in range(members + 1):
        u = jnp.where(edge, place_edges(packed, f, lane), inner_ref[f])
        if f < members:
            ens_out[f] = u
        else:
            static_out[...] = u


def on_device(
    control_ens,
    control_static,
    static_sigma,
    east_coef,
    north_coef,
    perturbations,
    obs_counts,
    obs_rows,
    footprints,
    obs_values,
    obs_precision,
):
    members, levels, latitudes, columns = control_ens.shape
    slots = perturbations.shape[1]
    rows = levels * latitudes
    table_rows = slots * rows
    groups = lax.axis_size("mem")
    scale = 1.0 / math.sqrt(members * groups - 1)
    ens = control_ens.reshape(members, rows, columns)
    static = control_static.reshape(rows, columns)
    sigma = static_sigma.reshape(rows, columns)
    e = east_coef.reshape(rows, columns)
    n = north_coef.reshape(rows, columns)
    pert = perturbations.reshape(members, slots, rows, columns)
    tiles, cap = obs_rows.shape[2:]

    field = shape((rows, columns))

    room = cap + 1
    wide = -(-RUN * room // 8) * 8
    runs, across = runs_of("tile")
    outer = len(runs)
    message, own = call(
        first_body,
        (shape((RUN, room * outer + rows, columns), BF16), field),
        1e6,
        1e6,
        footprints[0, 0],
        obs_counts[0],
        obs_rows[0, 0].T,
        obs_values[0, 0].T,
        obs_precision[0, 0].T,
        ens,
        static,
        e,
        n,
        spec=BLOCKS,
        limit=60,
        scratch=[pltpu.VMEM((tiles * 2 * cap, columns), F32)],
    )
    message = lax.all_to_all(message, "tile", 0, 0, axis_index_groups=runs, tiled=True)
    far = between_runs(own, "tile")
    x = (lax.axis_index("tile") % RUN).reshape(1)
    message, west, east = call(
        functools.partial(turn_body, room),
        (shape((outer, wide, columns), BF16), field, field),
        TURN,
        1e6,
        x,
        message,
        specs=[SCALAR, VMEM],
        scratch=[pltpu.VMEM((outer * wide, columns), F32)],
    )
    seen = lax.all_to_all(message, "tile", 0, 0, axis_index_groups=across, tiled=True)
    late, _ = lax.optimization_barrier((static, message))

    share = 1.0 / groups
    coded = shape((table_rows + TAIL, columns), jnp.int16)
    inner = call(
        lambda *refs: inner_increment_body(latitudes, scale, share, *refs),
        shape((table_rows, columns)),
        BESIDE,
        4e6,
        ens,
        late,
        sigma,
        e,
        n,
        pert,
    )
    partial, e_packed, n_packed = call(
        lambda *refs: outer_increment_body(latitudes, scale, share, *refs),
        (coded, field, field),
        4e9,
        4e6,
        x,
        inner,
        own,
        far,
        west,
        east,
        sigma,
        e,
        n,
        pert,
        specs=[SCALAR] + [VMEM] * 9,
    )
    parts = lax.all_gather(partial, "mem")
    partial_grad = call(
        lambda *refs: observe_body(cap, wide, *refs),
        coded,
        3e8,
        4e6,
        parts,
        seen.reshape(-1, columns),
    )
    grad_parts = lax.all_gather(partial_grad, "mem")
    source, own_source = call(
        lambda *refs: source_body(scale, *refs),
        (shape((members + 1, rows, columns)), field),
        1e7,
        2e6,
        grad_parts,
        pert,
        sigma,
    )
    west, east = from_neighbours(own_source.astype(BF16), "tile")
    inner = call(
        lambda *refs: inner_result_body(latitudes, *refs),
        shape(source.shape),
        BESIDE,
        4e6,
        source,
        ens,
        static,
        e,
        n,
    )
    ens_out, static_out = call(
        outer_result_body,
        (shape(ens.shape), field),
        1e7,
        2e6,
        inner,
        own_source,
        west,
        east,
        own,
        e_packed,
        n_packed,
    )
    return ens_out.reshape(control_ens.shape), static_out.reshape(control_static.shape)


def solution(mesh):
    placed = (
        P("mem", None, None, "tile"),
        P(None, None, "tile"),
        P(None, None, "tile"),
        P(None, None, "tile"),
        P(None, None, "tile"),
        P("mem", None, None, None, "tile"),
        P("mem", "tile", None),
        P("mem", "tile", None, None),
        P("mem", "tile", None, None, None),
        P("mem", "tile", None, None),
        P("mem", "tile", None, None),
    )
    return jax.shard_map(
        on_device,
        mesh=mesh,
        in_specs=placed,
        out_specs=(P("mem", None, None, "tile"), P(None, None, "tile")),
        check_vma=False,
    )
```
